512 devices in a mesh: ctx: 32 (over z, x), head: 16 (over y, core).
Axes of the slice: x: 4, y: 8, z: 8, core: 2. Of those that a mesh axis runs over, the one named last changes fastest.
Arguments:
- queries: bfloat16 [16384, 4096], P('ctx', 'head'), may hold values from -6 to 6
- keys: bfloat16 [2, 16384, 4096], P(None, 'ctx', 'head'), may hold values from -6 to 6
- values: bfloat16 [2, 16384, 4096], P(None, 'ctx', 'head'), may hold values from -6 to 6
- betas: float32 [32, 2, 16384], P('head', None, 'ctx'), may hold values from 1.9 to 2
- gate: bfloat16 [16384, 4096], P('ctx', 'head'), may hold values from -6 to 6
- out_weight: bfloat16 [4096, 4096], P('head'), may hold values from -0.125 to 0.125
Outputs:
- mixed: bfloat16 [16384, 4096], P('ctx', 'head')
The draws below stay inside these ranges and needn't reach their ends.
All inputs are finite; a program needn't handle non-finite values.
Results may differ from the reference program's by a relative error of at most 0.02.
Values may be sent and summed in bfloat16 or wider, within the bound.
No kernel may reach another device: no remote copies, remote signals or barrier semaphores. Data moves between devices by JAX's collectives and lax.ppermute only.
A program may use at most 64 MiB of HBM per device.

```python
import math
import jax
import jax.numpy as jnp
from jax import lax

D = 4096
HEADS = 32
HEAD_DIM = 128
SPAN = 64
TOKENS = 16384
N_HEAD = 16


def strengthened(values, own_key, source, target, parts, factor):
    owner, partner = [(jnp.arange(values.shape[dim]) // (values.shape[dim] // parts)).reshape([-1 if axis == dim else 1 for axis in range(values.ndim)]) for dim in (source, target)]
    chosen = jax.random.permutation(own_key, parts)[partner]
    strong = (owner == chosen) | (owner == (partner + parts // 2) % parts)
    return jnp.where(strong, factor * values, values)


def block_levels(key, shape, shards, low, largest):
    gain, own = 1.0, jax.random.fold_in(key, 6)
    for axis_at, blocks in shards:
        heights = jnp.exp(jax.random.uniform(jax.random.fold_in(own, axis_at), (blocks,), jnp.float32, low / len(shards), largest / len(shards)))
        gain = gain * jnp.repeat(heights, shape[axis_at] // blocks).reshape([-1 if axis == axis_at else 1 for axis in range(len(shape))])
    return gain


def scatter_about(key, extent, deviation, limit, shards=(), kind=jnp.bfloat16):
    loudness = block_levels(key, extent, shards, -0.22, 0.18) if shards else 1.0
    values = jax.random.normal(key, extent, jnp.float32) * deviation * loudness
    return jnp.minimum(jnp.maximum(values, -limit), limit).astype(kind)


def noise_with(key, shape, deviation, limit, cuts, heavy, kind=jnp.bfloat16):
    entries = deviation * jax.random.normal(key, shape, jnp.float32)
    if cuts:
        entries = entries * block_levels(key, shape, cuts, -0.22, 0.18)
    return jnp.clip(strengthened(entries, jax.random.fold_in(key, 3), *heavy), -limit, limit).astype(kind)


def setup_inputs(seed: int = 0) -> dict:
    key_list = jax.random.split(jax.random.key(seed), 7)
    return {
        "queries": scatter_about(key_list[0], (TOKENS, HEADS * HEAD_DIM), 1.0, 6.0, ((0, 32), (1, 16))),
        "keys": scatter_about(key_list[1], (2, TOKENS, HEADS * HEAD_DIM), 1.0, 6.0, ((1, 32), (2, 16))),
        "values": scatter_about(key_list[2], (2, TOKENS, HEADS * HEAD_DIM), 1.0, 6.0, ((1, 32), (2, 16))),
        "betas": jnp.clip(1.9 + 0.100000024 * jax.random.uniform(key_list[3], (HEADS, 2, TOKENS), jnp.float32) ** block_levels(key_list[3], (HEADS, 2, TOKENS), ((0, 16), (2, 32)), -0.2, 0.2), 1.9, 2.0),
        "gate": scatter_about(key_list[4], (TOKENS, HEADS * HEAD_DIM), 1.0, 6.0, ((0, 32), (1, 16))),
        "out_weight": noise_with(key_list[5], (HEADS * HEAD_DIM, D), (HEADS * HEAD_DIM) ** -0.5, 0.125, ((0, 16),), (0, 1, 16, 2.0)),
    }


def product(left, right_part):
    return jnp.matmul(left, right_part, precision=lax.Precision.HIGHEST)

def flipped(array):
    return jnp.swapaxes(array, -1, -2)

def unit_rows(array):
    array = array.astype(jnp.float32)
    return array * lax.rsqrt(lax.optimization_barrier(jnp.sum(array * array, axis=-1, keepdims=True)) + 1e-06)

def unit_lower_solve(system, right_side):
    order = system.shape[-1]
    width = math.gcd(16, order)
    eye_block = jnp.eye(width, dtype=jnp.float32)
    pieces = []
    for index in range(order // width):
        first = index * width
        rhs = right_side[..., first:first + width, :]
        if index > 0:
            rhs = rhs - product(system[..., first:first + width, :first], jnp.concatenate(pieces, axis=-2))
        lower = system[..., first:first + width, first:first + width] - eye_block
        inverse = eye_block - lower
        power = lower
        degree = 1
        while 2 * degree < width:
            power = product(power, power)
            inverse = product(inverse, eye_block + power)
            degree = 2 * degree
        pieces.append(product(inverse, rhs))
    return jnp.concatenate(pieces, axis=-2)

def block_factors(keys_c, values_c, betas_c, queries_c):
    sub_steps = keys_c.shape[-2]
    block_tokens = queries_c.shape[-2]
    head_size = keys_c.shape[-1]
    row_index = lax.broadcasted_iota(jnp.int32, (sub_steps, sub_steps), 0)
    col_index = lax.broadcasted_iota(jnp.int32, (sub_steps, sub_steps), 1)
    strict_lower = (col_index < row_index).astype(jnp.float32)
    system = jnp.eye(sub_steps, dtype=jnp.float32) + betas_c[..., :, None] * product(keys_c, flipped(keys_c)) * strict_lower
    right_side = betas_c[..., :, None] * jnp.concatenate([keys_c, values_c], axis=-1)
    solved = unit_lower_solve(system, right_side)
    mixing = solved[..., :head_size]
    updates = solved[..., head_size:]
    query_row = lax.broadcasted_iota(jnp.int32, (block_tokens, sub_steps), 0)
    key_col = lax.broadcasted_iota(jnp.int32, (block_tokens, sub_steps), 1)
    causal = (key_col <= 2 * query_row + 1).astype(jnp.float32)
    scores = product(queries_c, flipped(keys_c)) * causal
    local_out = product(scores, updates)
    carry_map = queries_c - product(scores, mixing)
    transit = jnp.eye(head_size, dtype=jnp.float32) - product(flipped(keys_c), mixing)
    source = product(flipped(keys_c), updates)
    return (local_out, carry_map, transit, source)

def reference(queries, keys, values, betas, gate, out_weight):
    blocks = TOKENS // SPAN
    query_seq = queries.reshape(blocks, SPAN, HEADS, HEAD_DIM).transpose(0, 2, 1, 3)
    key_seq = keys.reshape(2, blocks, SPAN, HEADS, HEAD_DIM).transpose(1, 3, 2, 0, 4).reshape(blocks, HEADS, 2 * SPAN, HEAD_DIM)
    value_seq = values.reshape(2, blocks, SPAN, HEADS, HEAD_DIM).transpose(1, 3, 2, 0, 4).reshape(blocks, HEADS, 2 * SPAN, HEAD_DIM)
    beta_seq = betas.reshape(HEADS, 2, blocks, SPAN).transpose(2, 0, 3, 1).reshape(blocks, HEADS, 2 * SPAN)

    def advance(state, pieces):
        query_c, key_c, value_c, beta_c = pieces
        local_out, carry_map, transit, source = block_factors(unit_rows(key_c), value_c.astype(jnp.float32), beta_c, unit_rows(query_c))
        return (product(transit, state) + source, local_out + product(carry_map, state))
    start = jnp.zeros((HEADS, HEAD_DIM, HEAD_DIM), jnp.float32)
    final_state, outputs = lax.scan(advance, start, (query_seq, key_seq, value_seq, beta_seq))
    attended = outputs.transpose(0, 2, 1, 3).reshape(TOKENS, HEADS, HEAD_DIM)
    scale = lax.rsqrt(lax.optimization_barrier(jnp.mean(attended * attended, axis=-1, keepdims=True)) + 1e-06)
    mixed_in = (attended * scale * jax.nn.silu(gate.astype(jnp.float32).reshape(TOKENS, HEADS, HEAD_DIM))).astype(jnp.bfloat16)
    mixed_in = mixed_in.reshape(TOKENS, HEADS * HEAD_DIM)
    group = HEADS * HEAD_DIM // N_HEAD

    def add_group(index, total):
        cols = lax.dynamic_slice_in_dim(mixed_in, index * group, group, 1)
        weight = lax.dynamic_slice_in_dim(out_weight, index * group, group, 0)
        part_sum = jnp.dot(cols, weight, preferred_element_type=jnp.float32).astype(jnp.bfloat16)
        part_sum = lax.optimization_barrier(part_sum)
        return total + part_sum.astype(jnp.float32)
    total = lax.fori_loop(0, N_HEAD, add_group, jnp.zeros((TOKENS, D), jnp.float32))
    return total.astype(jnp.bfloat16)
```

```python
import functools
import jax
import jax.numpy as jnp
from jax import lax
from jax.experimental import pallas as pl
from jax.experimental.pallas import tpu as pltpu
from jax.sharding import Mesh
from jax.sharding import PartitionSpec as P

F32 = jnp.float32
BF16 = jnp.bfloat16
HD = 128
SPAN = 64
CTX = ("ctx_0", "ctx_1")


def dot(a, b):
    return jnp.dot(a, b, preferred_element_type=F32)


def dot_nt(a, b):
    return lax.dot_general(a, b, (((1,), (1,)), ((), ())), preferred_element_type=F32)


def split(x):
    hi = x.astype(BF16)
    return hi, (x - hi.astype(F32)).astype(BF16)


def wide(x):
    return jnp.concatenate(split(x), axis=1)


def square(pair):
    return jnp.concatenate([pair, pair], axis=0)


def halves(x):
    n = x.shape[1] // 2
    return x[:, :n] + x[:, n:]


def local_kernel(group, q_ref, k_ref, v_ref, b_ref, ab_ref, l_ref, m_ref, lev_ref, p_ref):
    heads = q_ref.shape[1] // HD
    blocks = q_ref.shape[0] // SPAN
    sub = 2 * SPAN
    place_r = lax.broadcasted_iota(jnp.int32, (sub, sub), 0)
    place_c = lax.broadcasted_iota(jnp.int32, (sub, sub), 1)

    def order(p):
        return (p & ~31) + 2 * (p & 15) + ((p >> 4) & 1)

    s_r, s_c = order(place_r), order(place_c)
    apart = s_r ^ s_c
    level = jnp.zeros((sub, sub), jnp.int32)
    for bit in range(1, 7):
        level = level + (apart >= 2**bit).astype(jnp.int32)
    lev_ref[...] = jnp.where(s_r > s_c, level, -1)
    eye = (place_r == place_c).astype(F32)
    seen = (order(lax.broadcasted_iota(jnp.int32, (SPAN, sub), 1)) >> 1) <= lax.broadcasted_iota(
        jnp.int32, (SPAN, sub), 0
    )
    for h in range(heads):
        p_ref[h] = jnp.concatenate([eye, jnp.zeros((HD, HD), F32)], axis=1)

    def body(step, carry):
        probs = [(step * group + i, h) for i in range(group) for h in range(heads)]
        kb, vb, qb, sq, n, e, N, X = [], [], [], [], [], [], [], []
        for blk, h in probs:
            rows = [
                (j, pl.ds(pl.multiple_of(blk * SPAN + 16 * g, 16), 16))
                for g in range(SPAN // 16)
                for j in range(2)
            ]
            cols = slice(h * HD, (h + 1) * HD)
            kb.append(jnp.concatenate([k_ref[j, r, cols] for j, r in rows], axis=0))
            vb.append(jnp.concatenate([v_ref[j, r, cols] for j, r in rows], axis=0))
            qb.append(q_ref[pl.ds(pl.multiple_of(blk * SPAN, SPAN), SPAN), cols])
        num = range(len(probs))
        for i in num:
            blk, h = probs[i]
            both = dot_nt(jnp.concatenate([kb[i], qb[i]], axis=0), kb[i])
            gram = both[:sub]
            n2 = jnp.sum(gram * eye, axis=0, keepdims=True) + 1e-6
            beta = b_ref[pl.ds(h * blocks + blk, 1), :]
            e.append(beta / n2)
            n.append(jnp.sqrt(n2))
            sq.append((jnp.where(seen, both[sub:], 0.0) * e[i]).astype(BF16))
            N.append(jnp.where(lev_ref[...] >= 0, gram * e[i], 0.0))
            X.append(eye - jnp.where(lev_ref[...] == 0, N[i], 0.0))
        for lev in range(1, 7):
            xw = [wide(x) for x in X]
            Z = []
            for i in num:
                C = jnp.where(lev_ref[...] == lev, N[i], 0.0)
                Z.append(halves(dot(wide(C), square(xw[i]))))
            for i in num:
                X[i] = X[i] - halves(dot(xw[i], square(wide(Z[i]))))
        A, B, carry_q, loc = [], [], [], []
        for i in num:
            xw = wide(X[i])
            ke = wide(kb[i].T.astype(F32) * e[i])
            y = halves(dot(ke, square(xw)))
            A.append(eye - dot(wide(y), square(kb[i])))
            B.append(dot(wide(y * n[i]), square(vb[i])))
            zq = dot(sq[i], xw[:, :sub])
            carry_q.append((qb[i].astype(F32) - dot(zq.astype(BF16), kb[i])).astype(BF16))
            loc.append(dot((zq * n[i]).astype(BF16), vb[i]))
        for i in num:
            blk, h = probs[i]
            p = p_ref[h]
            ph, plo = split(p)
            lm = dot(carry_q[i], ph)
            rows = pl.ds(pl.multiple_of(blk * SPAN, SPAN), SPAN)
            cols = slice(h * HD, (h + 1) * HD)
            m_ref[rows, cols] = lm[:, :HD].astype(BF16)
            l_ref[rows, cols] = loc[i] + lm[:, HD:]
            aw = wide(A[i])
            new = dot(aw, square(ph)) + dot(aw[:, :HD], plo)
            p_ref[h] = new + jnp.concatenate([jnp.zeros((HD, HD), F32), B[i]], axis=1)
        return carry

    lax.fori_loop(0, blocks // group, body, 0)
    for h in range(heads):
        ab_ref[h] = p_ref[h].astype(BF16)


def local_maps(q, k, v, b_rows, group=2):
    tok, cols = q.shape
    heads = cols // HD
    return pl.pallas_call(
        functools.partial(local_kernel, group),
        out_shape=(
            jax.ShapeDtypeStruct((heads, HD, 2 * HD), BF16),
            jax.ShapeDtypeStruct((tok, cols), F32),
            jax.ShapeDtypeStruct((tok, cols), BF16),
        ),
        in_specs=[pl.BlockSpec(memory_space=pltpu.VMEM)] * 4,
        out_specs=[pl.BlockSpec(memory_space=pltpu.VMEM)] * 3,
        scratch_shapes=[
            pltpu.VMEM((2 * SPAN, 2 * SPAN), jnp.int32),
            pltpu.VMEM((heads, HD, 2 * HD), F32),
        ],
        compiler_params=pltpu.CompilerParams(vmem_limit_bytes=32 * 1024 * 1024),
    )(q, k, v, b_rows)


def beta_rows(betas):
    heads, _, tok = betas.shape
    blocks = tok // SPAN
    return (
        betas.reshape(heads, 2, blocks, SPAN // 16, 16)
        .transpose(0, 2, 3, 1, 4)
        .reshape(heads * blocks, 2 * SPAN)
    )


def affine(a, b):
    return jnp.concatenate([a, b], axis=1)


def fold_kernel(x_ref, m_ref, send_ref, tot_ref, in_ref):
    peers, heads = m_ref.shape[:2]
    x = x_ref[0]
    r = lax.broadcasted_iota(jnp.int32, (HD, 2 * HD), 0)
    c = lax.broadcasted_iota(jnp.int32, (HD, 2 * HD), 1)
    zero = jnp.zeros((HD, HD), F32)
    total = [m_ref[0, h].astype(F32) for h in range(heads)]
    inside = [(r == c).astype(F32)] * heads
    for k in range(1, peers):
        for h in range(heads):
            inside[h] = jnp.where(x == k, total[h], inside[h])
            later = m_ref[k, h]
            prod = halves(dot(later[:, :HD], jnp.concatenate(split(total[h]), axis=1)))
            total[h] = prod + affine(zero, later[:, HD:].astype(F32))
    for h in range(heads):
        send_ref[h] = total[h].astype(BF16)
        tot_ref[h] = total[h]
        in_ref[h] = inside[h]


def join_kernel(later_ref, earlier_ref, send_ref, out_ref):
    zero = jnp.zeros((HD, HD), F32)
    for h in range(later_ref.shape[0]):
        later = later_ref[h]
        out = dot(wide(later[:, :HD]), square(earlier_ref[h])) + affine(zero, later[:, HD:])
        send_ref[h] = out.astype(BF16)
        out_ref[h] = out


def carry_kernel(later_ref, earlier_ref, send_ref):
    for h in range(later_ref.shape[0]):
        later = later_ref[h]
        state = dot(wide(later[:, :HD]), square(earlier_ref[h][:, HD:])) + later[:, HD:]
        send_ref[h] = state.astype(BF16)


def entry_kernel(in_ref, near_ref, far_ref, out_ref):
    zero = jnp.zeros((HD, HD), F32)
    for h in range(in_ref.shape[0]):
        near = near_ref[h]
        both = dot(near[:, :HD], far_ref[h]) + affine(zero, near[:, HD:].astype(F32))
        inner = in_ref[h]
        bh, bl = split(both)
        lhs = wide(inner[:, :HD])
        out = dot(lhs, square(bh)) + dot(lhs[:, :HD], bl)
        out_ref[h] = out + affine(zero, inner[:, HD:])


def mix_kernel(entry_ref, state_ref, l_ref, m_ref, q_ref, g_ref, o_ref):
    for h in range(entry_ref.shape[0]):
        entry = entry_ref[h]
        start = dot(wide(entry[:, :HD]), square(state_ref[h])) + entry[:, HD:]
        cols = slice(h * HD, (h + 1) * HD)
        raw = l_ref[:, cols] + dot(m_ref[:, cols], start.astype(BF16))
        q = q_ref[:, cols].astype(F32)
        unit = lax.rsqrt(jnp.sum(q * q, axis=1, keepdims=True) + 1e-6)
        mean = jnp.mean(raw * raw, axis=1, keepdims=True) * (unit * unit)
        gate = g_ref[:, cols].astype(F32)
        silu = gate / (1.0 + jnp.exp(-gate))
        o_ref[:, cols] = (raw * (unit * lax.rsqrt(mean + 1e-6)) * silu).astype(BF16)


VM = pl.BlockSpec(memory_space=pltpu.VMEM)
SM = pl.BlockSpec(memory_space=pltpu.SMEM)


def small(kernel, outs, *args, specs=None):
    return pl.pallas_call(
        kernel,
        out_shape=outs,
        in_specs=specs or [VM] * len(args),
        out_specs=jax.tree.map(lambda _: VM, outs),
        compiler_params=pltpu.CompilerParams(vmem_limit_bytes=32 * 1024 * 1024),
    )(*args)


def project_kernel(own_at, mate_at, a_ref, b_ref, w_ref, x_ref, o_ref):
    o_ref[0] = (dot(a_ref[...], w_ref[...]) + dot(b_ref[...], x_ref[...])).astype(o_ref.dtype)


def project(own, mate, weight, mate_weight, own_at, mate_at):
    tok, cols = own.shape
    count = own_at.shape[0]
    full = pl.BlockSpec((tok, cols), lambda i, a, b: (0, 0))
    return pl.pallas_call(
        project_kernel,
        out_shape=jax.ShapeDtypeStruct((count, tok, cols), BF16),
        grid_spec=pltpu.PrefetchScalarGridSpec(
            num_scalar_prefetch=2,
            grid=(count,),
            in_specs=[
                full,
                full,
                pl.BlockSpec((cols, cols), lambda i, a, b: (0, a[i])),
                pl.BlockSpec((cols, cols), lambda i, a, b: (0, b[i])),
            ],
            out_specs=pl.BlockSpec((1, tok, cols), lambda i, a, b: (i, 0, 0)),
        ),
        compiler_params=pltpu.CompilerParams(vmem_limit_bytes=32 * 1024 * 1024),
    )(own_at, mate_at, own, mate, weight, mate_weight)


def per_device(queries, keys, values, betas, gate, out_weight):
    tok, cols = queries.shape
    heads = cols // HD
    devices = lax.axis_size("head")
    chips = devices // 2
    me = lax.axis_index("head")
    chip, core = me // 2, me % 2

    def shift(a, by):
        return lax.ppermute(a, "head", [(i, (i + 2 * by) % devices) for i in range(devices)])

    def mate(a):
        return lax.ppermute(a, "head", [(i, i ^ 1) for i in range(devices)])

    def later_z(a, by):
        groups = lax.axis_size("ctx_0")
        return lax.ppermute(a, "ctx_0", [(i, i + by) for i in range(groups - by)])

    maps, local, carry = local_maps(queries, keys, values, beta_rows(betas), 8)
    to_mate = lax.dynamic_index_in_dim(
        out_weight.reshape(cols, chips, 2, cols), 1 - core, 2, keepdims=False
    ).reshape(cols, chips * cols)
    mate_weight = mate(to_mate)

    wide_map = jax.ShapeDtypeStruct((heads, HD, 2 * HD), F32)
    wide_send = jax.ShapeDtypeStruct((heads, HD, 2 * HD), BF16)
    state_send = jax.ShapeDtypeStruct((heads, HD, HD), BF16)
    gathered = lax.all_gather(maps, "ctx_1")
    x = lax.axis_index("ctx_1").astype(jnp.int32).reshape(1)
    send, total, inside = small(
        fold_kernel, (wide_send, wide_map, wide_map), x, gathered, specs=[SM, VM]
    )
    near = later_z(send, 1)
    send, pair = small(join_kernel, (wide_send, wide_map), total, near)
    far = later_z(send, 2)
    send = small(carry_kernel, state_send, pair, far)
    state = later_z(send, 4)
    entry = small(entry_kernel, wide_map, inside, near, far)
    mixed_in = small(
        mix_kernel,
        jax.ShapeDtypeStruct((tok, cols), BF16),
        entry,
        state,
        local,
        carry,
        queries,
        gate,
    )
    mate_in = mate(mixed_in)

    half = chips // 2
    order = [half] + [s for k in range(half - 1, 0, -1) for s in (k, chips - k)] + [0]
    dest = (chip + jnp.array(order, jnp.int32)) % chips
    own_at, mate_at = 2 * dest + core, dest
    first = project(mixed_in, mate_in, out_weight, mate_weight, own_at[:1], mate_at[:1])[0]
    rest = project(mixed_in, mate_in, out_weight, mate_weight, own_at[1:], mate_at[1:])
    cut = tok // 2
    up = shift(first[:cut], 1)
    down = shift(first[cut:], -1)

    def add(*terms):
        return sum(t.astype(F32) for t in terms).astype(BF16)

    up = jnp.concatenate([add(rest[0, :cut], up), rest[0, cut:]], axis=0)
    down = jnp.concatenate([rest[1, :cut], add(rest[1, cut:], down)], axis=0)
    for k in range(1, half):
        up, down = shift(up, 1), shift(down, -1)
        if k < half - 1:
            up, down = add(rest[2 * k], up), add(rest[2 * k + 1], down)
    return add(rest[2 * half - 2], up, down)


def solution(mesh):
    z = mesh.shape["ctx"] // 4
    finer = Mesh(mesh.devices.reshape(z, 4, mesh.shape["head"]), ("ctx_0", "ctx_1", "head"))
    in_specs = (
        P(CTX, "head"),
        P(None, CTX, "head"),
        P(None, CTX, "head"),
        P("head", None, CTX),
        P(CTX, "head"),
        P("head", None),
    )
    return jax.shard_map(
        per_device, mesh=finer, in_specs=in_specs, out_specs=P(CTX, "head"), check_vma=False
    )
```

```python
import functools
import jax
import jax.numpy as jnp
from jax import lax
from jax.experimental import pallas as pl
from jax.experimental.pallas import tpu as pltpu
from jax.sharding import Mesh
from jax.sharding import PartitionSpec as P

F32 = jnp.float32
BF16 = jnp.bfloat16
HD = 128
SPAN = 64
CTX = ("ctx_0", "ctx_1")


def dot(a, b):
    return jnp.dot(a, b, preferred_element_type=F32)


def dot_nt(a, b):
    return lax.dot_general(a, b, (((1,), (1,)), ((), ())), preferred_element_type=F32)


def split(x):
    hi = x.astype(BF16)
    return hi, (x - hi.astype(F32)).astype(BF16)


def wide(x):
    return jnp.concatenate(split(x), axis=1)


def square(pair):
    return jnp.concatenate([pair, pair], axis=0)


def halves(x):
    n = x.shape[1] // 2
    return x[:, :n] + x[:, n:]


def read_block(ref, blk, h):
    rows = [
        (j, pl.ds(pl.multiple_of(blk * SPAN + 16 * g, 16), 16))
        for g in range(SPAN // 16)
        for j in range(2)
    ]
    cols = slice(h * HD, (h + 1) * HD)
    return jnp.concatenate([ref[j, r, cols] for j, r in rows], axis=0)


def order(p):
    return (p & ~31) + 2 * (p & 15) + ((p >> 4) & 1)


def map_kernel(
    group, k_hbm, v_hbm, b_ref, ab_ref, x_ref, e_ref, pre_ref, k_ref, v_ref, lev_ref, p_ref, sems
):
    get_k = pltpu.make_async_copy(k_hbm, k_ref, sems.at[0])
    get_v = pltpu.make_async_copy(v_hbm, v_ref, sems.at[1])
    get_k.start()
    get_v.start()
    heads = k_ref.shape[2] // HD
    blocks = k_ref.shape[1] // SPAN
    sub = 2 * SPAN
    place_r = lax.broadcasted_iota(jnp.int32, (sub, sub), 0)
    place_c = lax.broadcasted_iota(jnp.int32, (sub, sub), 1)
    s_r, s_c = order(place_r), order(place_c)
    apart = s_r ^ s_c
    level = jnp.zeros((sub, sub), jnp.int32)
    for bit in range(1, 7):
        level = level + (apart >= 2**bit).astype(jnp.int32)
    lev_ref[...] = jnp.where(s_r > s_c, level, -1)
    eye = (place_r == place_c).astype(F32)
    for h in range(heads):
        p_ref[h] = jnp.concatenate([eye, jnp.zeros((HD, HD), F32)], axis=1)
    get_k.wait()
    get_v.wait()

    def body(step, carry):
        probs = [(step * group + i, h) for i in range(group) for h in range(heads)]
        kb = [read_block(k_ref, blk, h) for blk, h in probs]
        num = range(len(probs))
        n, e, N, X = [], [], [], []
        for i in num:
            blk, h = probs[i]
            gram = dot_nt(kb[i], kb[i])
            n2 = jnp.sum(gram * eye, axis=0, keepdims=True) + 1e-6
            e.append(b_ref[pl.ds(h * blocks + blk, 1), :] / n2)
            n.append(jnp.sqrt(n2))
            e_ref[h * blocks + blk] = jnp.concatenate([e[i], n[i]], axis=0)
            N.append(jnp.where(lev_ref[...] >= 0, gram * e[i], 0.0))
            X.append(eye - jnp.where(lev_ref[...] == 0, N[i], 0.0))
        for lev in range(1, 7):
            xw = [wide(x) for x in X]
            Z = []
            for i in num:
                C = jnp.where(lev_ref[...] == lev, N[i], 0.0)
                Z.append(halves(dot(wide(C), square(xw[i]))))
            for i in num:
                X[i] = X[i] - halves(dot(xw[i], square(wide(Z[i]))))
        A, B = [], []
        for i in num:
            blk, h = probs[i]
            xw = wide(X[i])
            x_ref[h * blocks + blk] = xw
            ke = wide(kb[i].T.astype(F32) * e[i])
            y = halves(dot(ke, square(xw)))
            A.append(wide(eye - dot(wide(y), square(kb[i]))))
            B.append(dot(wide(y * n[i]), square(read_block(v_ref, blk, h))))
        for i in num:
            blk, h = probs[i]
            p = p_ref[h]
            ph, plo = split(p)
            pre_ref[h * blocks + blk] = ph
            new = dot(A[i], square(ph)) + dot(A[i][:, :HD], plo)
            p_ref[h] = new + jnp.concatenate([jnp.zeros((HD, HD), F32), B[i]], axis=1)
        return carry

    lax.fori_loop(0, blocks // group, body, 0)
    for h in range(heads):
        ab_ref[h] = p_ref[h].astype(BF16)


def local_maps(k, v, b_rows, group):
    _, tok, cols = k.shape
    heads = cols // HD
    count = heads * tok // SPAN
    return pl.pallas_call(
        functools.partial(map_kernel, group),
        out_shape=(
            jax.ShapeDtypeStruct((heads, HD, 2 * HD), BF16),
            jax.ShapeDtypeStruct((count, 2 * SPAN, 4 * SPAN), BF16),
            jax.ShapeDtypeStruct((count, 2, 2 * SPAN), F32),
            jax.ShapeDtypeStruct((count, HD, 2 * HD), BF16),
        ),
        in_specs=[pl.BlockSpec(memory_space=pltpu.HBM)] * 2 + [pl.BlockSpec(memory_space=pltpu.VMEM)],
        out_specs=[pl.BlockSpec(memory_space=pltpu.VMEM)] * 4,
        scratch_shapes=[
            pltpu.VMEM(k.shape, k.dtype),
            pltpu.VMEM(v.shape, v.dtype),
            pltpu.VMEM((2 * SPAN, 2 * SPAN), jnp.int32),
            pltpu.VMEM((heads, HD, 2 * HD), F32),
            pltpu.SemaphoreType.DMA((2,)),
        ],
        compiler_params=pltpu.CompilerParams(vmem_limit_bytes=32 * 1024 * 1024),
    )(k, v, b_rows)


def local_kernel(q_ref, k_ref, v_ref, g_ref, x_ref, e_ref, pre_ref, l_ref, m_ref, s_ref):
    heads = q_ref.shape[1] // HD
    blocks = q_ref.shape[0] // SPAN
    sub = 2 * SPAN
    seen = (order(lax.broadcasted_iota(jnp.int32, (SPAN, sub), 1)) >> 1) <= lax.broadcasted_iota(
        jnp.int32, (SPAN, sub), 0
    )
    spots = [
        (h * blocks + blk, slice(blk * SPAN, (blk + 1) * SPAN), slice(h * HD, (h + 1) * HD))
        for blk in range(blocks)
        for h in range(heads)
    ]
    num = range(len(spots))
    kb = [read_block(k_ref, i // heads, i % heads) for i in num]
    scores = [
        wide(jnp.where(seen, dot_nt(q_ref[rows, cols], kb[i]), 0.0) * e_ref[at, :1])
        for i, (at, rows, cols) in enumerate(spots)
    ]
    zq = [halves(dot(scores[i], square(x_ref[spots[i][0]]))) for i in num]
    carry = [
        (q_ref[rows, cols].astype(F32) - dot(wide(zq[i]), square(kb[i]))).astype(BF16)
        for i, (_, rows, cols) in enumerate(spots)
    ]
    loc = [
        dot(wide(zq[i] * e_ref[spots[i][0], 1:]), square(read_block(v_ref, i // heads, i % heads)))
        for i in num
    ]
    prod = [dot(carry[i], pre_ref[spots[i][0]]) for i in num]
    for i, (_, rows, cols) in enumerate(spots):
        qf = q_ref[rows, cols].astype(F32)
        unit = lax.rsqrt(jnp.sum(qf * qf, axis=1, keepdims=True) + 1e-6)
        m_ref[rows, cols] = (prod[i][:, :HD] * unit).astype(BF16)
        l_ref[rows, cols] = (loc[i] + prod[i][:, HD:]) * unit
        gate = g_ref[rows, cols].astype(F32)
        s_ref[rows, cols] = gate / (1.0 + jnp.exp(-gate))


def beta_rows(betas):
    heads, _, tok = betas.shape
    blocks = tok // SPAN
    return (
        betas.reshape(heads, 2, blocks, SPAN // 16, 16)
        .transpose(0, 2, 3, 1, 4)
        .reshape(heads * blocks, 2 * SPAN)
    )


def affine(a, b):
    return jnp.concatenate([a, b], axis=1)


def fold_kernel(x_ref, m_ref, send_ref, tot_ref, in_ref):
    peers, heads = m_ref.shape[:2]
    x = x_ref[0]
    r = lax.broadcasted_iota(jnp.int32, (HD, 2 * HD), 0)
    c = lax.broadcasted_iota(jnp.int32, (HD, 2 * HD), 1)
    zero = jnp.zeros((HD, HD), F32)
    total = [m_ref[0, h].astype(F32) for h in range(heads)]
    inside = [(r == c).astype(F32)] * heads
    for k in range(1, peers):
        for h in range(heads):
            inside[h] = jnp.where(x == k, total[h], inside[h])
            later = m_ref[k, h]
            prod = halves(dot(later[:, :HD], jnp.concatenate(split(total[h]), axis=1)))
            total[h] = prod + affine(zero, later[:, HD:].astype(F32))
    for h in range(heads):
        send_ref[h] = total[h].astype(BF16)
        tot_ref[h] = total[h]
        in_ref[h] = inside[h]


def join_kernel(later_ref, earlier_ref, send_ref, out_ref):
    zero = jnp.zeros((HD, HD), F32)
    for h in range(later_ref.shape[0]):
        later = later_ref[h]
        out = dot(wide(later[:, :HD]), square(earlier_ref[h])) + affine(zero, later[:, HD:])
        send_ref[h] = out.astype(BF16)
        out_ref[h] = out


def carry_kernel(later_ref, earlier_ref, send_ref):
    for h in range(later_ref.shape[0]):
        later = later_ref[h]
        state = dot(wide(later[:, :HD]), square(earlier_ref[h][:, HD:])) + later[:, HD:]
        send_ref[h] = state.astype(BF16)


def entry_kernel(in_ref, near_ref, far_ref, out_ref):
    zero = jnp.zeros((HD, HD), F32)
    for h in range(in_ref.shape[0]):
        near = near_ref[h]
        both = dot(near[:, :HD], far_ref[h]) + affine(zero, near[:, HD:].astype(F32))
        inner = in_ref[h]
        bh, bl = split(both)
        lhs = wide(inner[:, :HD])
        out = dot(lhs, square(bh)) + dot(lhs[:, :HD], bl)
        out_ref[h] = out + affine(zero, inner[:, HD:])


def mix_kernel(entry_ref, state_ref, l_ref, m_ref, s_ref, o_ref):
    for h in range(entry_ref.shape[0]):
        entry = entry_ref[h]
        start = dot(wide(entry[:, :HD]), square(state_ref[h])) + entry[:, HD:]
        cols = slice(h * HD, (h + 1) * HD)
        att = l_ref[:, cols] + dot(m_ref[:, cols], start.astype(BF16))
        scale = lax.rsqrt(jnp.mean(att * att, axis=1, keepdims=True) + 1e-6)
        o_ref[:, cols] = (att * scale * s_ref[:, cols]).astype(BF16)


VM = pl.BlockSpec(memory_space=pltpu.VMEM)
SM = pl.BlockSpec(memory_space=pltpu.SMEM)


def small(kernel, outs, *args, specs=None):
    return pl.pallas_call(
        kernel,
        out_shape=outs,
        in_specs=specs or [VM] * len(args),
        out_specs=jax.tree.map(lambda _: VM, outs),
        compiler_params=pltpu.CompilerParams(vmem_limit_bytes=32 * 1024 * 1024),
    )(*args)


def term(at, a_ref, b_ref, w_ref, x_ref):
    width = a_ref.shape[1]
    cols = pl.ds(pl.multiple_of(at * width, width), width)
    return dot(a_ref[...], w_ref[:, cols]) + dot(b_ref[...], x_ref[:, cols])


def far_kernel(at_ref, a_ref, b_ref, w_ref, x_ref, up_ref, down_ref):
    out = term(at_ref[0], a_ref, b_ref, w_ref, x_ref).astype(BF16)
    up_ref[...] = out[: up_ref.shape[0]]
    down_ref[...] = out[up_ref.shape[0] :]


def terms_kernel(at_ref, a_ref, b_ref, w_ref, x_ref, o_ref):
    for i in range(o_ref.shape[0]):
        o_ref[i] = term(at_ref[i], a_ref, b_ref, w_ref, x_ref)


def first_add_kernel(at, rows, terms_ref, got_ref, o_ref):
    o_ref[...] = terms_ref[at].astype(BF16)
    o_ref[rows] = (terms_ref[at, rows] + got_ref[...].astype(F32)).astype(BF16)


def add_kernel(at, terms_ref, got_ref, o_ref):
    o_ref[...] = (terms_ref[at] + got_ref[...].astype(F32)).astype(o_ref.dtype)


def last_add_kernel(a_ref, b_ref, o_ref):
    o_ref[...] = (a_ref[...] + b_ref[...].astype(F32)).astype(BF16)


def per_device(queries, keys, values, betas, gate, out_weight):
    tok, cols = queries.shape
    heads = cols // HD
    devices = lax.axis_size("head")
    chips = devices // 2
    me = lax.axis_index("head")
    chip, core = me // 2, me % 2

    def shift(a, by):
        return lax.ppermute(a, "head", [(i, (i + 2 * by) % devices) for i in range(devices)])

    def mate(a):
        return lax.ppermute(a, "head", [(i, i ^ 1) for i in range(devices)])

    def later_z(a, by):
        groups = lax.axis_size("ctx_0")
        return lax.ppermute(a, "ctx_0", [(i, i + by) for i in range(groups - by)])

    mate_weight = mate(out_weight)
    maps, inverse, scales, prefixes = local_maps(keys, values, beta_rows(betas), 8)

    wide_map = jax.ShapeDtypeStruct((heads, HD, 2 * HD), F32)
    wide_send = jax.ShapeDtypeStruct((heads, HD, 2 * HD), BF16)
    state_send = jax.ShapeDtypeStruct((heads, HD, HD), BF16)
    gathered = lax.all_gather(maps, "ctx_1")
    x = lax.axis_index("ctx_1").astype(jnp.int32).reshape(1)
    send, total, inside = small(
        fold_kernel, (wide_send, wide_map, wide_map), x, gathered, specs=[SM, VM]
    )
    near = later_z(send, 1)
    send, pair = small(join_kernel, (wide_send, wide_map), total, near)
    far = later_z(send, 2)
    tokens = jax.ShapeDtypeStruct((tok, cols), F32)
    local, carry, silu = small(
        local_kernel,
        (tokens, jax.ShapeDtypeStruct((tok, cols), BF16), tokens),
        queries,
        keys,
        values,
        gate,
        inverse,
        scales,
        lax.optimization_barrier((prefixes, near))[0],
    )
    send = small(carry_kernel, state_send, pair, far)
    state = later_z(send, 4)
    entry = small(entry_kernel, wide_map, inside, near, far)
    mixed_in = small(
        mix_kernel,
        jax.ShapeDtypeStruct((tok, cols), BF16),
        entry,
        state,
        local,
        carry,
        silu,
    )
    mate_in = mate(mixed_in)

    half = chips // 2
    sides = [s for k in range(half - 1, 0, -1) for s in (k, chips - k)] + [0]
    at = [2 * ((chip + jnp.array(o, jnp.int32)) % chips) + core for o in ([half], sides)]

    weights = (mixed_in, mate_in, out_weight, mate_weight)
    specs = [SM] + [VM] * 4
    cut = tok // 2
    part = jax.ShapeDtypeStruct((cut, cols), BF16)
    up, down = small(far_kernel, (part, part), at[0], *weights, specs=specs)
    up, down = shift(up, 1), shift(down, -1)
    several = jax.ShapeDtypeStruct((len(sides), tok, cols), F32)
    terms = small(terms_kernel, several, at[1], *weights, specs=specs)
    sent = jax.ShapeDtypeStruct((tok, cols), BF16)
    down_sum = None
    for k in range(half - 1):
        adders = [functools.partial(add_kernel, 2 * k + i) for i in range(2)]
        if k == 0:
            adders = [
                functools.partial(first_add_kernel, i, r)
                for i, r in enumerate((slice(0, cut), slice(cut, tok)))
            ]
        else:
            up = lax.optimization_barrier((up, down_sum))[0]
        up_sum = small(adders[0], sent, terms, up)
        down = lax.optimization_barrier((down, up_sum))[0]
        down_sum = small(adders[1], sent, terms, down)
        up, down = shift(up_sum, 1), shift(down_sum, -1)
    last = functools.partial(add_kernel, 2 * half - 2)
    up = lax.optimization_barrier((up, down_sum))[0]
    total = small(last, tokens, terms, up)
    return small(last_add_kernel, sent, total, down)


def solution(mesh):
    z = mesh.shape["ctx"] // 4
    finer = Mesh(mesh.devices.reshape(z, 4, mesh.shape["head"]), ("ctx_0", "ctx_1", "head"))
    in_specs = (
        P(CTX, "head"),
        P(None, CTX, "head"),
        P(None, CTX, "head"),
        P("head", None, CTX),
        P(CTX, "head"),
        P("head", None),
    )
    return jax.shard_map(
        per_device, mesh=finer, in_specs=in_specs, out_specs=P(CTX, "head"), check_vma=False
    )
```

```python
import functools
import jax
import jax.numpy as jnp
from jax import lax
from jax.experimental import pallas as pl
from jax.experimental.pallas import tpu as pltpu
from jax.sharding import Mesh
from jax.sharding import PartitionSpec as P

F32 = jnp.float32
BF16 = jnp.bfloat16
HD = 128
SPAN = 64
CTX = ("ctx_0", "ctx_1")


def dot(a, b):
    return jnp.dot(a, b, preferred_element_type=F32)


def dot_nt(a, b):
    return lax.dot_general(a, b, (((1,), (1,)), ((), ())), preferred_element_type=F32)


def split(x):
    hi = x.astype(BF16)
    return hi, (x - hi.astype(F32)).astype(BF16)


def wide(x):
    return jnp.concatenate(split(x), axis=1)


def square(pair):
    return jnp.concatenate([pair, pair], axis=0)


def halves(x):
    n = x.shape[1] // 2
    return x[:, :n] + x[:, n:]


def read_block(ref, blk, h):
    rows = [
        (j, pl.ds(pl.multiple_of(blk * SPAN + 16 * g, 16), 16))
        for g in range(SPAN // 16)
        for j in range(2)
    ]
    cols = slice(h * HD, (h + 1) * HD)
    return jnp.concatenate([ref[j, r, cols] for j, r in rows], axis=0)


def order(p):
    return (p & ~31) + 2 * (p & 15) + ((p >> 4) & 1)


def map_kernel(
    group, k_hbm, v_hbm, b_ref, ab_ref, x_ref, e_ref, pre_ref, k_ref, v_ref, lev_ref, p_ref, sems
):
    get_k = pltpu.make_async_copy(k_hbm, k_ref, sems.at[0])
    get_v = pltpu.make_async_copy(v_hbm, v_ref, sems.at[1])
    get_k.start()
    get_v.start()
    heads = k_ref.shape[2] // HD
    blocks = k_ref.shape[1] // SPAN
    sub = 2 * SPAN
    place_r = lax.broadcasted_iota(jnp.int32, (sub, sub), 0)
    place_c = lax.broadcasted_iota(jnp.int32, (sub, sub), 1)
    s_r, s_c = order(place_r), order(place_c)
    apart = s_r ^ s_c
    level = jnp.zeros((sub, sub), jnp.int32)
    for bit in range(1, 7):
        level = level + (apart >= 2**bit).astype(jnp.int32)
    lev_ref[...] = jnp.where(s_r > s_c, level, -1)
    eye = (place_r == place_c).astype(F32)
    for h in range(heads):
        p_ref[h] = jnp.concatenate([eye, jnp.zeros((HD, HD), F32)], axis=1)
    get_k.wait()
    get_v.wait()

    def body(step, carry):
        probs = [(step * group + i, h) for i in range(group) for h in range(heads)]
        kb = [read_block(k_ref, blk, h) for blk, h in probs]
        num = range(len(probs))
        n, e, N, X = [], [], [], []
        for i in num:
            blk, h = probs[i]
            gram = dot_nt(kb[i], kb[i])
            n2 = jnp.sum(gram * eye, axis=0, keepdims=True) + 1e-6
            e.append(b_ref[pl.ds(h * blocks + blk, 1), :] / n2)
            n.append(jnp.sqrt(n2))
            e_ref[h * blocks + blk] = jnp.concatenate([e[i], n[i]], axis=0)
            N.append(jnp.where(lev_ref[...] >= 0, gram * e[i], 0.0))
            X.append(eye - jnp.where(lev_ref[...] == 0, N[i], 0.0))
        for lev in range(1, 7):
            xw = [wide(x) for x in X]
            Z = []
            for i in num:
                C = jnp.where(lev_ref[...] == lev, N[i], 0.0)
                Z.append(halves(dot(wide(C), square(xw[i]))))
            for i in num:
                X[i] = X[i] - halves(dot(xw[i], square(wide(Z[i]))))
        A, B = [], []
        for i in num:
            blk, h = probs[i]
            xw = wide(X[i])
            x_ref[h * blocks + blk] = xw
            ke = wide(kb[i].T.astype(F32) * e[i])
            y = halves(dot(ke, square(xw)))
            A.append(wide(eye - dot(wide(y), square(kb[i]))))
            B.append(dot(wide(y * n[i]), square(read_block(v_ref, blk, h))))
        for i in num:
            blk, h = probs[i]
            p = p_ref[h]
            ph, plo = split(p)
            pre_ref[h * blocks + blk] = ph
            new = dot(A[i], square(ph)) + dot(A[i][:, :HD], plo)
            p_ref[h] = new + jnp.concatenate([jnp.zeros((HD, HD), F32), B[i]], axis=1)
        return carry

    lax.fori_loop(0, blocks // group, body, 0)
    for h in range(heads):
        ab_ref[h] = p_ref[h].astype(BF16)


def local_maps(k, v, b_rows, group):
    _, tok, cols = k.shape
    heads = cols // HD
    count = heads * tok // SPAN
    return pl.pallas_call(
        functools.partial(map_kernel, group),
        out_shape=(
            jax.ShapeDtypeStruct((heads, HD, 2 * HD), BF16),
            jax.ShapeDtypeStruct((count, 2 * SPAN, 4 * SPAN), BF16),
            jax.ShapeDtypeStruct((count, 2, 2 * SPAN), F32),
            jax.ShapeDtypeStruct((count, HD, 2 * HD), BF16),
        ),
        in_specs=[pl.BlockSpec(memory_space=pltpu.HBM)] * 2 + [pl.BlockSpec(memory_space=pltpu.VMEM)],
        out_specs=[pl.BlockSpec(memory_space=pltpu.VMEM)] * 4,
        scratch_shapes=[
            pltpu.VMEM(k.shape, k.dtype),
            pltpu.VMEM(v.shape, v.dtype),
            pltpu.VMEM((2 * SPAN, 2 * SPAN), jnp.int32),
            pltpu.VMEM((heads, HD, 2 * HD), F32),
            pltpu.SemaphoreType.DMA((2,)),
        ],
        compiler_params=pltpu.CompilerParams(vmem_limit_bytes=32 * 1024 * 1024),
    )(*(pltpu.with_memory_space_constraint(a, pltpu.HBM) for a in (k, v)), b_rows)


def local_kernel(q_ref, k_ref, v_ref, g_ref, x_ref, e_ref, pre_ref, l_ref, m_ref, s_ref):
    heads = q_ref.shape[1] // HD
    blocks = q_ref.shape[0] // SPAN
    sub = 2 * SPAN
    seen = (order(lax.broadcasted_iota(jnp.int32, (SPAN, sub), 1)) >> 1) <= lax.broadcasted_iota(
        jnp.int32, (SPAN, sub), 0
    )
    spots = [
        (h * blocks + blk, slice(blk * SPAN, (blk + 1) * SPAN), slice(h * HD, (h + 1) * HD))
        for blk in range(blocks)
        for h in range(heads)
    ]
    num = range(len(spots))
    kb = [read_block(k_ref, i // heads, i % heads) for i in num]
    scores = [
        wide(jnp.where(seen, dot_nt(q_ref[rows, cols], kb[i]), 0.0) * e_ref[at, :1])
        for i, (at, rows, cols) in enumerate(spots)
    ]
    zq = [halves(dot(scores[i], square(x_ref[spots[i][0]]))) for i in num]
    carry = [
        (q_ref[rows, cols].astype(F32) - dot(wide(zq[i]), square(kb[i]))).astype(BF16)
        for i, (_, rows, cols) in enumerate(spots)
    ]
    loc = [
        dot(wide(zq[i] * e_ref[spots[i][0], 1:]), square(read_block(v_ref, i // heads, i % heads)))
        for i in num
    ]
    prod = [dot(carry[i], pre_ref[spots[i][0]]) for i in num]
    for i, (_, rows, cols) in enumerate(spots):
        qf = q_ref[rows, cols].astype(F32)
        unit = lax.rsqrt(jnp.sum(qf * qf, axis=1, keepdims=True) + 1e-6)
        m_ref[rows, cols] = (prod[i][:, :HD] * unit).astype(BF16)
        l_ref[rows, cols] = (loc[i] + prod[i][:, HD:]) * unit
        gate = g_ref[rows, cols].astype(F32)
        s_ref[rows, cols] = gate / (1.0 + jnp.exp(-gate))


def beta_rows(betas):
    heads, _, tok = betas.shape
    blocks = tok // SPAN
    return (
        betas.reshape(heads, 2, blocks, SPAN // 16, 16)
        .transpose(0, 2, 3, 1, 4)
        .reshape(heads * blocks, 2 * SPAN)
    )


def affine(a, b):
    return jnp.concatenate([a, b], axis=1)


def fold_kernel(x_ref, m_ref, send_ref, tot_ref, in_ref):
    peers, heads = m_ref.shape[:2]
    x = x_ref[0]
    r = lax.broadcasted_iota(jnp.int32, (HD, 2 * HD), 0)
    c = lax.broadcasted_iota(jnp.int32, (HD, 2 * HD), 1)
    zero = jnp.zeros((HD, HD), F32)
    total = [m_ref[0, h].astype(F32) for h in range(heads)]
    inside = [(r == c).astype(F32)] * heads
    for k in range(1, peers):
        for h in range(heads):
            inside[h] = jnp.where(x == k, total[h], inside[h])
            later = m_ref[k, h]
            prod = halves(dot(later[:, :HD], jnp.concatenate(split(total[h]), axis=1)))
            total[h] = prod + affine(zero, later[:, HD:].astype(F32))
    for h in range(heads):
        send_ref[h] = total[h].astype(BF16)
        tot_ref[h] = total[h]
        in_ref[h] = inside[h]


def join_kernel(later_ref, earlier_ref, send_ref, out_ref):
    zero = jnp.zeros((HD, HD), F32)
    for h in range(later_ref.shape[0]):
        later = later_ref[h]
        out = dot(wide(later[:, :HD]), square(earlier_ref[h])) + affine(zero, later[:, HD:])
        send_ref[h] = out.astype(BF16)
        out_ref[h] = out


def carry_kernel(later_ref, earlier_ref, send_ref):
    for h in range(later_ref.shape[0]):
        later = later_ref[h]
        state = dot(wide(later[:, :HD]), square(earlier_ref[h][:, HD:])) + later[:, HD:]
        send_ref[h] = state.astype(BF16)


def entry_kernel(in_ref, near_ref, far_ref, out_ref):
    zero = jnp.zeros((HD, HD), F32)
    for h in range(in_ref.shape[0]):
        near = near_ref[h]
        both = dot(near[:, :HD], far_ref[h]) + affine(zero, near[:, HD:].astype(F32))
        inner = in_ref[h]
        bh, bl = split(both)
        lhs = wide(inner[:, :HD])
        out = dot(lhs, square(bh)) + dot(lhs[:, :HD], bl)
        out_ref[h] = out + affine(zero, inner[:, HD:])


def mix_kernel(entry_ref, state_ref, l_ref, m_ref, s_ref, o_ref):
    for h in range(entry_ref.shape[0]):
        entry = entry_ref[h]
        start = dot(wide(entry[:, :HD]), square(state_ref[h])) + entry[:, HD:]
        cols = slice(h * HD, (h + 1) * HD)
        att = l_ref[:, cols] + dot(m_ref[:, cols], start.astype(BF16))
        scale = lax.rsqrt(jnp.mean(att * att, axis=1, keepdims=True) + 1e-6)
        o_ref[:, cols] = (att * scale * s_ref[:, cols]).astype(BF16)


VM = pl.BlockSpec(memory_space=pltpu.VMEM)
SM = pl.BlockSpec(memory_space=pltpu.SMEM)


def small(kernel, outs, *args, specs=None):
    return pl.pallas_call(
        kernel,
        out_shape=outs,
        in_specs=specs or [VM] * len(args),
        out_specs=jax.tree.map(lambda _: VM, outs),
        compiler_params=pltpu.CompilerParams(vmem_limit_bytes=32 * 1024 * 1024),
    )(*args)


def term(at, a_ref, b_ref, w_ref, x_ref):
    width = a_ref.shape[1]
    cols = pl.ds(pl.multiple_of(at * width, width), width)
    return dot(a_ref[...], w_ref[:, cols]) + dot(b_ref[...], x_ref[:, cols])


def far_kernel(at_ref, a_ref, b_ref, w_ref, x_ref, ahead_ref, back_ref):
    out = term(at_ref[0], a_ref, b_ref, w_ref, x_ref).astype(BF16)
    cut = ahead_ref.shape[0]
    flip = at_ref[1] != 0
    ahead_ref[...] = jnp.where(flip, out[cut:], out[:cut])
    back_ref[...] = jnp.where(flip, out[:cut], out[cut:])


def terms_kernel(at_ref, a_ref, b_ref, w_ref, x_ref, o_ref):
    for i in range(o_ref.shape[0]):
        o_ref[i] = term(at_ref[i], a_ref, b_ref, w_ref, x_ref)


def first_add_kernel(at, odd_ref, terms_ref, got_ref, o_ref):
    cut = got_ref.shape[0]
    low = odd_ref[0] == at
    for i in range(2):
        rows = slice(i * cut, (i + 1) * cut)
        mine = low if i == 0 else jnp.logical_not(low)
        got = jnp.where(mine, got_ref[...].astype(F32), 0.0)
        o_ref[rows] = (terms_ref[at, rows] + got).astype(BF16)


def add_kernel(at, terms_ref, got_ref, o_ref):
    o_ref[...] = (terms_ref[at] + got_ref[...].astype(F32)).astype(o_ref.dtype)


def last_add_kernel(a_ref, b_ref, o_ref):
    o_ref[...] = (a_ref[...] + b_ref[...].astype(F32)).astype(BF16)


def per_device(queries, keys, values, betas, gate, out_weight):
    tok, cols = queries.shape
    heads = cols // HD
    devices = lax.axis_size("head")
    chips = devices // 2
    me = lax.axis_index("head")
    chip, core = me // 2, me % 2

    def across(a, odd):
        pairs = [(c, (c + 1) % chips) for c in range(odd, chips, 2)]
        both = pairs + [(d, c) for c, d in pairs]
        return lax.ppermute(a, "head", [(2 * c + i, 2 * d + i) for c, d in both for i in range(2)])

    def mate(a):
        return lax.ppermute(a, "head", [(i, i ^ 1) for i in range(devices)])

    def later_z(a, by):
        groups = lax.axis_size("ctx_0")
        return lax.ppermute(a, "ctx_0", [(i, i + by) for i in range(groups - by)])

    mate_weight = mate(out_weight)
    maps, inverse, scales, prefixes = local_maps(keys, values, beta_rows(betas), 8)

    wide_map = jax.ShapeDtypeStruct((heads, HD, 2 * HD), F32)
    wide_send = jax.ShapeDtypeStruct((heads, HD, 2 * HD), BF16)
    state_send = jax.ShapeDtypeStruct((heads, HD, HD), BF16)
    gathered = lax.all_gather(maps, "ctx_1")
    x = lax.axis_index("ctx_1").astype(jnp.int32).reshape(1)
    send, total, inside = small(
        fold_kernel, (wide_send, wide_map, wide_map), x, gathered, specs=[SM, VM]
    )
    near = later_z(send, 1)
    send, pair = small(join_kernel, (wide_send, wide_map), total, near)
    far = later_z(send, 2)
    tokens = jax.ShapeDtypeStruct((tok, cols), F32)
    local, carry, silu = small(
        local_kernel,
        (tokens, jax.ShapeDtypeStruct((tok, cols), BF16), tokens),
        queries,
        keys,
        values,
        gate,
        inverse,
        scales,
        lax.optimization_barrier((prefixes, near))[0],
    )
    send = small(carry_kernel, state_send, pair, far)
    mate_weight, far = lax.optimization_barrier((mate_weight, far))
    state = later_z(send, 4)
    entry = small(entry_kernel, wide_map, inside, near, far)
    mixed_in = small(
        mix_kernel,
        jax.ShapeDtypeStruct((tok, cols), BF16),
        entry,
        state,
        local,
        carry,
        silu,
    )
    mate_in = mate(mixed_in)

    half = chips // 2
    odd = chip % 2
    sign = 1 - 2 * odd
    sides = [s for k in range(half - 1, 0, -1) for s in (k, -k)] + [0]
    at = 2 * ((chip + chips + sign * jnp.array(sides, jnp.int32)) % chips) + core
    far_at = jnp.stack([2 * ((chip + half) % chips) + core, odd]).astype(jnp.int32)
    odd = odd.astype(jnp.int32).reshape(1)

    weights = (mixed_in, mate_in, out_weight, mate_weight)
    specs = [SM] + [VM] * 4
    part = jax.ShapeDtypeStruct((tok // 2, cols), BF16)
    ahead, back = small(far_kernel, (part, part), far_at, *weights, specs=specs)
    back, ahead = across(ahead, 0), across(back, 1)
    several = jax.ShapeDtypeStruct((len(sides), tok, cols), F32)
    terms = small(terms_kernel, several, at, *weights, specs=specs)
    sent = jax.ShapeDtypeStruct((tok, cols), BF16)
    arrived, prior = {0: ahead, 1: back}, None
    for k in range(half):
        sums = {}
        for i in (1, 0) if k % 2 == 0 else (0, 1):
            got = arrived[i]
            if prior is not None:
                got = lax.optimization_barrier((got, prior))[0]
            if k == 0:
                adder = functools.partial(first_add_kernel, i)
                sums[i] = small(adder, sent, odd, terms, got, specs=[SM, VM, VM])
            elif k < half - 1:
                sums[i] = small(functools.partial(add_kernel, 2 * k + i), sent, terms, got)
            elif not sums:
                sums[i] = small(functools.partial(add_kernel, 2 * k), tokens, terms, got)
            else:
                return small(last_add_kernel, sent, prior, got)
            prior = sums[i]
        arrived = {0: across(sums[1], 1), 1: across(sums[0], 0)}


def solution(mesh):
    z = mesh.shape["ctx"] // 4
    finer = Mesh(mesh.devices.reshape(z, 4, mesh.shape["head"]), ("ctx_0", "ctx_1", "head"))
    in_specs = (
        P(CTX, "head"),
        P(None, CTX, "head"),
        P(None, CTX, "head"),
        P("head", None, CTX),
        P(CTX, "head"),
        P("head", None),
    )
    return jax.shard_map(
        per_device, mesh=finer, in_specs=in_specs, out_specs=P(CTX, "head"), check_vma=False
    )
```

```python
import functools
import jax
import jax.numpy as jnp
from jax import lax
from jax.experimental import pallas as pl
from jax.experimental.pallas import tpu as pltpu
from jax.sharding import Mesh
from jax.sharding import PartitionSpec as P

F32 = jnp.float32
BF16 = jnp.bfloat16
HD = 128
SPAN = 64
CTX = ("ctx_0", "ctx_1")


def dot(a, b):
    return jnp.dot(a, b, preferred_element_type=F32)


def dot_nt(a, b):
    return lax.dot_general(a, b, (((1,), (1,)), ((), ())), preferred_element_type=F32)


def split(x):
    hi = x.astype(BF16)
    return hi, (x - hi.astype(F32)).astype(BF16)


def wide(x):
    return jnp.concatenate(split(x), axis=1)


def square(pair):
    return jnp.concatenate([pair, pair], axis=0)


def halves(x):
    n = x.shape[1] // 2
    return x[:, :n] + x[:, n:]


def read_block(ref, blk, h):
    rows = [
        (j, pl.ds(pl.multiple_of(blk * SPAN + 16 * g, 16), 16))
        for g in range(SPAN // 16)
        for j in range(2)
    ]
    cols = slice(h * HD, (h + 1) * HD)
    return jnp.concatenate([ref[j, r, cols] for j, r in rows], axis=0)


def order(p):
    return (p & ~31) + 2 * (p & 15) + ((p >> 4) & 1)


def map_kernel(
    group, k_hbm, v_hbm, b_ref, ab_ref, x_ref, e_ref, pre_ref, k_ref, v_ref, lev_ref, p_ref, sems
):
    get_k = pltpu.make_async_copy(k_hbm, k_ref, sems.at[0])
    get_v = pltpu.make_async_copy(v_hbm, v_ref, sems.at[1])
    get_k.start()
    get_v.start()
    heads = k_ref.shape[2] // HD
    blocks = k_ref.shape[1] // SPAN
    sub = 2 * SPAN
    place_r = lax.broadcasted_iota(jnp.int32, (sub, sub), 0)
    place_c = lax.broadcasted_iota(jnp.int32, (sub, sub), 1)
    s_r, s_c = order(place_r), order(place_c)
    apart = s_r ^ s_c
    level = jnp.zeros((sub, sub), jnp.int32)
    for bit in range(1, 7):
        level = level + (apart >= 2**bit).astype(jnp.int32)
    lev_ref[...] = jnp.where(s_r > s_c, level, -1)
    eye = (place_r == place_c).astype(F32)
    for h in range(heads):
        p_ref[h] = jnp.concatenate([eye, jnp.zeros((HD, HD), F32)], axis=1)
    get_k.wait()
    get_v.wait()

    for step in range(blocks // group):
        probs = [(step * group + i, h) for i in range(group) for h in range(heads)]
        kb = [read_block(k_ref, blk, h) for blk, h in probs]
        num = range(len(probs))
        n, e, N, X = [], [], [], []
        for i in num:
            blk, h = probs[i]
            gram = dot_nt(kb[i], kb[i])
            n2 = jnp.sum(gram * eye, axis=0, keepdims=True) + 1e-6
            first = blk * SPAN
            beta = jnp.concatenate(
                [
                    b_ref[h, j : j + 1, first + 16 * g : first + 16 * (g + 1)]
                    for g in range(SPAN // 16)
                    for j in range(2)
                ],
                axis=1,
            )
            e.append(beta / n2)
            n.append(jnp.sqrt(n2))
            e_ref[h * blocks + blk] = jnp.concatenate([e[i], n[i]], axis=0)
            N.append(jnp.where(lev_ref[...] >= 0, gram * e[i], 0.0))
            X.append(eye - jnp.where(lev_ref[...] == 0, N[i], 0.0))
        for lev in range(1, 7):
            xw = [wide(x) for x in X]
            Z = []
            for i in num:
                C = jnp.where(lev_ref[...] == lev, N[i], 0.0)
                Z.append(halves(dot(wide(C), square(xw[i]))))
            for i in num:
                X[i] = X[i] - halves(dot(xw[i], square(wide(Z[i]))))
        A, B = [], []
        for i in num:
            blk, h = probs[i]
            xw = wide(X[i])
            x_ref[h * blocks + blk] = xw
            ke = wide(kb[i].T.astype(F32) * e[i])
            y = halves(dot(ke, square(xw)))
            A.append(wide(eye - dot(wide(y), square(kb[i]))))
            B.append(dot(wide(y * n[i]), square(read_block(v_ref, blk, h))))
        for i in num:
            blk, h = probs[i]
            p = p_ref[h]
            ph, plo = split(p)
            pre_ref[h * blocks + blk] = ph
            new = dot(A[i], square(ph)) + dot(A[i][:, :HD], plo)
            p_ref[h] = new + jnp.concatenate([jnp.zeros((HD, HD), F32), B[i]], axis=1)
    for h in range(heads):
        ab_ref[h] = p_ref[h].astype(BF16)


def local_maps(k, v, betas, group):
    _, tok, cols = k.shape
    heads = cols // HD
    count = heads * tok // SPAN
    return pl.pallas_call(
        functools.partial(map_kernel, group),
        out_shape=(
            jax.ShapeDtypeStruct((heads, HD, 2 * HD), BF16),
            jax.ShapeDtypeStruct((count, 2 * SPAN, 4 * SPAN), BF16),
            jax.ShapeDtypeStruct((count, 2, 2 * SPAN), F32),
            jax.ShapeDtypeStruct((count, HD, 2 * HD), BF16),
        ),
        in_specs=[pl.BlockSpec(memory_space=pltpu.HBM)] * 2 + [pl.BlockSpec(memory_space=pltpu.VMEM)],
        out_specs=[pl.BlockSpec(memory_space=pltpu.VMEM)] * 4,
        scratch_shapes=[
            pltpu.VMEM(k.shape, k.dtype),
            pltpu.VMEM(v.shape, v.dtype),
            pltpu.VMEM((2 * SPAN, 2 * SPAN), jnp.int32),
            pltpu.VMEM((heads, HD, 2 * HD), F32),
            pltpu.SemaphoreType.DMA((2,)),
        ],
        compiler_params=pltpu.CompilerParams(vmem_limit_bytes=16 * 1024 * 1024),
    )(*(pltpu.with_memory_space_constraint(a, pltpu.HBM) for a in (k, v)), betas)


def local_kernel(q_ref, k_ref, v_ref, g_ref, x_ref, e_ref, pre_ref, l_ref, m_ref, s_ref):
    heads = q_ref.shape[1] // HD
    blocks = q_ref.shape[0] // SPAN
    sub = 2 * SPAN
    seen = (order(lax.broadcasted_iota(jnp.int32, (SPAN, sub), 1)) >> 1) <= lax.broadcasted_iota(
        jnp.int32, (SPAN, sub), 0
    )
    spots = [
        (h * blocks + blk, slice(blk * SPAN, (blk + 1) * SPAN), slice(h * HD, (h + 1) * HD))
        for blk in range(blocks)
        for h in range(heads)
    ]
    num = range(len(spots))
    kb = [read_block(k_ref, i // heads, i % heads) for i in num]
    scores = [
        wide(jnp.where(seen, dot_nt(q_ref[rows, cols], kb[i]), 0.0) * e_ref[at, :1])
        for i, (at, rows, cols) in enumerate(spots)
    ]
    zq = [halves(dot(scores[i], square(x_ref[spots[i][0]]))) for i in num]
    carry = [
        (q_ref[rows, cols].astype(F32) - dot(wide(zq[i]), square(kb[i]))).astype(BF16)
        for i, (_, rows, cols) in enumerate(spots)
    ]
    loc = [
        dot(wide(zq[i] * e_ref[spots[i][0], 1:]), square(read_block(v_ref, i // heads, i % heads)))
        for i in num
    ]
    prod = [dot(carry[i], pre_ref[spots[i][0]]) for i in num]
    for i, (_, rows, cols) in enumerate(spots):
        qf = q_ref[rows, cols].astype(F32)
        unit = lax.rsqrt(jnp.sum(qf * qf, axis=1, keepdims=True) + 1e-6)
        m_ref[rows, cols] = (prod[i][:, :HD] * unit).astype(BF16)
        l_ref[rows, cols] = (loc[i] + prod[i][:, HD:]) * unit
        gate = g_ref[rows, cols].astype(F32)
        s_ref[rows, cols] = gate / (1.0 + jnp.exp(-gate))


def affine(a, b):
    return jnp.concatenate([a, b], axis=1)


def fold_kernel(x_ref, m_ref, send_ref, tot_ref, in_ref):
    peers, heads = m_ref.shape[:2]
    x = x_ref[0]
    mine = x % heads
    r = lax.broadcasted_iota(jnp.int32, (HD, 2 * HD), 0)
    c = lax.broadcasted_iota(jnp.int32, (HD, 2 * HD), 1)
    zero = jnp.zeros((HD, HD), F32)

    def after(total, later):
        prod = halves(dot(later[:, :HD], jnp.concatenate(split(total), axis=1)))
        return prod + affine(zero, later[:, HD:].astype(F32))

    total = [m_ref[0, h].astype(F32) for h in range(heads)]
    inside = [(r == c).astype(F32)] * heads
    for k in range(1, peers):
        for h in range(heads):
            inside[h] = jnp.where(x == k, total[h], inside[h])
        if k < peers - 1:
            total = [after(total[h], m_ref[k, h]) for h in range(heads)]
    own = total[0]
    for h in range(1, heads):
        own = jnp.where(mine == h, total[h], own)
    own = after(own, m_ref[peers - 1, mine])
    send_ref[...] = own.astype(BF16)
    tot_ref[...] = own
    for h in range(heads):
        in_ref[h] = inside[h]


def join_kernel(later_ref, earlier_ref, send_ref, out_ref):
    later = later_ref[...]
    zero = jnp.zeros((HD, HD), F32)
    out = dot(wide(later[:, :HD]), square(earlier_ref[...])) + affine(zero, later[:, HD:])
    send_ref[...] = out.astype(BF16)
    out_ref[...] = out


def carry_kernel(later_ref, earlier_ref, send_ref):
    later = later_ref[...]
    earlier = earlier_ref[...]
    state = dot(wide(later[:, :HD]), square(earlier[:, -HD:])) + later[:, HD:]
    send_ref[...] = state.astype(BF16)


def entry_kernel(near_ref, far_ref, out_ref):
    near = near_ref[...]
    zero = jnp.zeros((HD, HD), F32)
    out_ref[...] = dot(near[:, :HD], far_ref[...]) + affine(zero, near[:, HD:].astype(F32))


def mix_kernel(x_ref, in_ref, own_ref, other_ref, l_ref, m_ref, s_ref, o_ref):
    heads = in_ref.shape[0]
    mine = x_ref[0] % heads
    for h in range(heads):
        state = jnp.where(mine == h, own_ref[...].astype(F32), other_ref[...].astype(F32))
        inner = in_ref[h]
        start = dot(wide(inner[:, :HD]), square(state.astype(BF16))) + inner[:, HD:]
        cols = slice(h * HD, (h + 1) * HD)
        att = l_ref[:, cols] + dot(m_ref[:, cols], start.astype(BF16))
        scale = lax.rsqrt(jnp.mean(att * att, axis=1, keepdims=True) + 1e-6)
        o_ref[:, cols] = (att * scale * s_ref[:, cols]).astype(BF16)


VM = pl.BlockSpec(memory_space=pltpu.VMEM)
SM = pl.BlockSpec(memory_space=pltpu.SMEM)


def small(kernel, outs, *args, specs=None):
    return pl.pallas_call(
        kernel,
        out_shape=outs,
        in_specs=specs or [VM] * len(args),
        out_specs=jax.tree.map(lambda _: VM, outs),
        compiler_params=pltpu.CompilerParams(vmem_limit_bytes=16 * 1024 * 1024),
    )(*args)


def pack_kernel(chips, me_ref, w_ref, x_ref, ring_ref, own_ref, sems):
    rows, width = w_ref.shape[0], own_ref.shape[1]
    count = ring_ref.shape[0]
    chip, core = me_ref[0] // 2, me_ref[0] % 2
    copies = []

    def put(ref, at, cols):
        block = pl.ds(pl.multiple_of(at * width, width), width)
        for j, source in enumerate((w_ref, x_ref)):
            target = ref.at[j * rows : (j + 1) * rows, cols]
            copies.append(pltpu.make_async_copy(source.at[:, block], target, sems.at[len(copies)]))
            copies[-1].start()

    for i in range(count):
        dest = (chip + chips + (1 - 2 * core) * (count - i)) % chips
        put(ring_ref.at[i], 2 * dest + core, slice(0, width))
        put(ring_ref.at[i], 2 * dest + 1 - core, slice(width, 2 * width))
    put(own_ref, me_ref[0], slice(0, width))
    for copy in copies:
        copy.wait()


def pack(chips, count, me, weight, mate_weight):
    rows = weight.shape[0]
    return pl.pallas_call(
        functools.partial(pack_kernel, chips),
        out_shape=(
            jax.ShapeDtypeStruct((count, 2 * rows, 2 * rows), BF16),
            jax.ShapeDtypeStruct((2 * rows, rows), BF16),
        ),
        in_specs=[SM] + [pl.BlockSpec(memory_space=pltpu.HBM)] * 2,
        out_specs=(VM, VM),
        scratch_shapes=[pltpu.SemaphoreType.DMA((4 * count + 2,))],
        compiler_params=pltpu.CompilerParams(vmem_limit_bytes=16 * 1024 * 1024),
    )(me, *(pltpu.with_memory_space_constraint(a, pltpu.HBM) for a in (weight, mate_weight)))


def term(a, b, w):
    rows = a.shape[1]
    return dot(a, w[:rows]) + dot(b, w[rows:])


def far_kernel(core_ref, a_ref, b_ref, w_ref, o_ref):
    cut = o_ref.shape[0]
    rows = pl.ds(pl.multiple_of(core_ref[0] * cut, cut), cut)
    o_ref[...] = term(a_ref[rows, :], b_ref[rows, :], w_ref[0]).astype(BF16)


def next_kernel(a_ref, b_ref, w_ref, o_ref):
    o_ref[...] = term(a_ref[...], b_ref[...], w_ref[1])


def rest_kernel(a_ref, b_ref, w_ref, own_w_ref, o_ref, own_ref):
    for i in range(o_ref.shape[0]):
        o_ref[i] = term(a_ref[...], b_ref[...], w_ref[2 + i])
    own_ref[...] = term(a_ref[...], b_ref[...], own_w_ref[...])


def first_add_kernel(core_ref, term_ref, got_ref, o_ref):
    cut = got_ref.shape[0]
    for i in range(2):
        rows = slice(i * cut, (i + 1) * cut)
        got = jnp.where(core_ref[0] == i, got_ref[...].astype(F32), 0.0)
        o_ref[rows] = (term_ref[rows] + got).astype(BF16)


def add_kernel(at, terms_ref, got_ref, *out_refs):
    width = out_refs[0].shape[1]
    for i, o_ref in enumerate(out_refs):
        cols = slice(i * width, (i + 1) * width)
        o_ref[...] = (terms_ref[at, :, cols] + got_ref[:, cols].astype(F32)).astype(BF16)


def last_add_kernel(a_ref, b_ref, c_ref, o_ref):
    o_ref[...] = (a_ref[...] + b_ref[...].astype(F32) + c_ref[...].astype(F32)).astype(BF16)


def per_device(queries, keys, values, betas, gate, out_weight):
    tok, cols = queries.shape
    heads = cols // HD
    devices = lax.axis_size("head")
    chips = devices // 2
    me = lax.axis_index("head")
    core = me % 2

    def onward(a, cross):
        hop = [
            (2 * c + i, 2 * ((c + 1 - 2 * i) % chips) + (i ^ cross)) for c in range(chips) for i in (0, 1)
        ]
        return lax.ppermute(a, "head", hop)

    def mate(a):
        return lax.ppermute(a, "head", [(i, i ^ 1) for i in range(devices)])

    def later_z(a, by):
        groups = lax.axis_size("ctx_0")
        return lax.ppermute(a, "ctx_0", [(i, i + by) for i in range(groups - by)])

    mate_weight = mate(out_weight)
    maps, inverse, scales, prefixes = local_maps(keys, values, betas, 8)

    wide_map = jax.ShapeDtypeStruct((HD, 2 * HD), F32)
    wide_send = jax.ShapeDtypeStruct((HD, 2 * HD), BF16)
    state_send = jax.ShapeDtypeStruct((HD, HD), BF16)
    inside_map = jax.ShapeDtypeStruct((heads, HD, 2 * HD), F32)
    tokens = jax.ShapeDtypeStruct((tok, cols), F32)
    sent = jax.ShapeDtypeStruct((tok, cols), BF16)

    gathered = lax.all_gather(maps, "ctx_1")
    x = lax.axis_index("ctx_1").astype(jnp.int32).reshape(1)
    send, total, inside = small(
        fold_kernel, (wide_send, wide_map, inside_map), x, gathered, specs=[SM, VM]
    )
    near = later_z(send, 1)
    send, pair = small(join_kernel, (wide_send, wide_map), total, near)
    far = later_z(send, 2)
    local, carry, silu = small(
        local_kernel,
        (tokens, sent, tokens),
        queries,
        keys,
        values,
        gate,
        inverse,
        scales,
        lax.optimization_barrier((prefixes, near))[0],
    )
    half = chips // 2
    ring_w, own_w = pack(
        chips,
        half,
        me.astype(jnp.int32).reshape(1),
        out_weight,
        lax.optimization_barrier((mate_weight, near))[0],
    )
    send = small(carry_kernel, state_send, pair, far)
    last = later_z(send, 4)
    entry = small(entry_kernel, wide_map, near, far)
    entry = lax.optimization_barrier((entry, silu, own_w))[0]
    own_state = small(carry_kernel, state_send, entry, last)
    peers = lax.axis_size("ctx_1")
    other_state = lax.ppermute(own_state, "ctx_1", [(i, i ^ 1) for i in range(peers)])
    mixed_in = small(
        mix_kernel,
        sent,
        x,
        inside,
        own_state,
        other_state,
        local,
        carry,
        silu,
        specs=[SM] + [VM] * 6,
    )
    mate_in = mate(mixed_in)

    which = core.astype(jnp.int32).reshape(1)
    got = small(
        far_kernel,
        jax.ShapeDtypeStruct((tok // 2, 2 * cols), BF16),
        which,
        mixed_in,
        mate_in,
        ring_w,
        specs=[SM] + [VM] * 3,
    )
    got = onward(got, 0)
    broad = jax.ShapeDtypeStruct((tok, 2 * cols), BF16)
    third = small(
        next_kernel, jax.ShapeDtypeStruct((tok, 2 * cols), F32), mixed_in, mate_in, ring_w
    )
    acc = small(first_add_kernel, broad, which, third, got, specs=[SM, VM, VM])
    rest, own = small(
        rest_kernel,
        (jax.ShapeDtypeStruct((half - 2, tok, 2 * cols), F32), tokens),
        lax.optimization_barrier((mixed_in, acc))[0],
        mate_in,
        ring_w,
        own_w,
    )
    for k in range(half - 3):
        acc = small(functools.partial(add_kernel, k), broad, rest, onward(acc, 0))
    got = onward(acc, 0)
    same, cross = small(functools.partial(add_kernel, half - 3), (sent, sent), rest, got)
    return small(last_add_kernel, sent, own, onward(same, 0), onward(cross, 1))


def solution(mesh):
    z = mesh.shape["ctx"] // 4
    finer = Mesh(mesh.devices.reshape(z, 4, mesh.shape["head"]), ("ctx_0", "ctx_1", "head"))
    in_specs = (
        P(CTX, "head"),
        P(None, CTX, "head"),
        P(None, CTX, "head"),
        P("head", None, CTX),
        P(CTX, "head"),
        P("head", None),
    )
    return jax.shard_map(
        per_device, mesh=finer, in_specs=in_specs, out_specs=P(CTX, "head"), check_vma=False
    )
```

```python
import functools
import jax
import jax.numpy as jnp
from jax import lax
from jax.experimental import pallas as pl
from jax.experimental.pallas import tpu as pltpu
from jax.sharding import Mesh
from jax.sharding import PartitionSpec as P

F32 = jnp.float32
BF16 = jnp.bfloat16
HD = 128
SPAN = 64
CTX = ("ctx_0", "ctx_1")


def dot(a, b):
    return jnp.dot(a, b, preferred_element_type=F32)


def dot_nt(a, b):
    return lax.dot_general(a, b, (((1,), (1,)), ((), ())), preferred_element_type=F32)


def split(x):
    hi = x.astype(BF16)
    return hi, (x - hi.astype(F32)).astype(BF16)


def wide(x):
    return jnp.concatenate(split(x), axis=1)


def square(pair):
    return jnp.concatenate([pair, pair], axis=0)


def halves(x):
    n = x.shape[1] // 2
    return x[:, :n] + x[:, n:]


def read_block(ref, blk, h):
    rows = [
        (j, pl.ds(pl.multiple_of(blk * SPAN + 16 * g, 16), 16))
        for g in range(SPAN // 16)
        for j in range(2)
    ]
    cols = slice(h * HD, (h + 1) * HD)
    return jnp.concatenate([ref[j, r, cols] for j, r in rows], axis=0)


def order(p):
    return (p & ~31) + 2 * (p & 15) + ((p >> 4) & 1)


def map_kernel(
    group, k_hbm, v_hbm, b_hbm, ab_ref, x_ref, e_ref, pre_ref, k_ref, v_ref, b_ref, lev_ref, p_ref, sems
):
    get_k = pltpu.make_async_copy(k_hbm, k_ref, sems.at[0])
    get_v = pltpu.make_async_copy(v_hbm, v_ref, sems.at[1])
    get_b = pltpu.make_async_copy(b_hbm, b_ref, sems.at[2])
    get_k.start()
    get_b.start()
    get_v.start()
    heads = k_ref.shape[2] // HD
    blocks = k_ref.shape[1] // SPAN
    sub = 2 * SPAN
    place_r = lax.broadcasted_iota(jnp.int32, (sub, sub), 0)
    place_c = lax.broadcasted_iota(jnp.int32, (sub, sub), 1)
    s_r, s_c = order(place_r), order(place_c)
    apart = s_r ^ s_c
    level = jnp.zeros((sub, sub), jnp.int32)
    for bit in range(1, 7):
        level = level + (apart >= 2**bit).astype(jnp.int32)
    lev_ref[...] = jnp.where(s_r > s_c, level, -1)
    eye = (place_r == place_c).astype(F32)
    for h in range(heads):
        p_ref[h] = jnp.concatenate([eye, jnp.zeros((HD, HD), F32)], axis=1)
    get_b.wait()
    get_k.wait()
    get_v.wait()

    for step in range(blocks // group):
        probs = [(step * group + i, h) for i in range(group) for h in range(heads)]
        kb = [read_block(k_ref, blk, h) for blk, h in probs]
        num = range(len(probs))
        n, e, N, X = [], [], [], []
        for i in num:
            blk, h = probs[i]
            gram = dot_nt(kb[i], kb[i])
            n2 = jnp.sum(gram * eye, axis=0, keepdims=True) + 1e-6
            first = blk * SPAN
            beta = jnp.concatenate(
                [
                    b_ref[h, j : j + 1, first + 16 * g : first + 16 * (g + 1)]
                    for g in range(SPAN // 16)
                    for j in range(2)
                ],
                axis=1,
            )
            e.append(beta / n2)
            n.append(jnp.sqrt(n2))
            e_ref[h * blocks + blk] = jnp.concatenate([e[i], n[i]], axis=0)
            N.append(jnp.where(lev_ref[...] >= 0, gram * e[i], 0.0))
            X.append(eye - jnp.where(lev_ref[...] == 0, N[i], 0.0))
        for lev in range(1, 7):
            xw = [wide(x) for x in X]
            Z = []
            for i in num:
                C = jnp.where(lev_ref[...] == lev, N[i], 0.0)
                Z.append(halves(dot(wide(C), square(xw[i]))))
            for i in num:
                X[i] = X[i] - halves(dot(xw[i], square(wide(Z[i]))))
        A, B = [], []
        for i in num:
            blk, h = probs[i]
            xw = wide(X[i])
            x_ref[h * blocks + blk] = xw
            ke = wide(kb[i].T.astype(F32) * e[i])
            y = halves(dot(ke, square(xw)))
            A.append(wide(eye - dot(wide(y), square(kb[i]))))
            B.append(dot(wide(y * n[i]), square(read_block(v_ref, blk, h))))
        for i in num:
            blk, h = probs[i]
            p = p_ref[h]
            ph, plo = split(p)
            pre_ref[h * blocks + blk] = ph
            new = dot(A[i], square(ph)) + dot(A[i][:, :HD], plo)
            p_ref[h] = new + jnp.concatenate([jnp.zeros((HD, HD), F32), B[i]], axis=1)
    for h in range(heads):
        ab_ref[h] = p_ref[h].astype(BF16)


def local_maps(k, v, betas, group):
    _, tok, cols = k.shape
    heads = cols // HD
    count = heads * tok // SPAN
    return pl.pallas_call(
        functools.partial(map_kernel, group),
        out_shape=(
            jax.ShapeDtypeStruct((heads, HD, 2 * HD), BF16),
            jax.ShapeDtypeStruct((count, 2 * SPAN, 4 * SPAN), BF16),
            jax.ShapeDtypeStruct((count, 2, 2 * SPAN), F32),
            jax.ShapeDtypeStruct((count, HD, 2 * HD), BF16),
        ),
        in_specs=[pl.BlockSpec(memory_space=pltpu.HBM)] * 3,
        out_specs=[pl.BlockSpec(memory_space=pltpu.VMEM)] * 4,
        scratch_shapes=[
            pltpu.VMEM(k.shape, k.dtype),
            pltpu.VMEM(v.shape, v.dtype),
            pltpu.VMEM(betas.shape, betas.dtype),
            pltpu.VMEM((2 * SPAN, 2 * SPAN), jnp.int32),
            pltpu.VMEM((heads, HD, 2 * HD), F32),
            pltpu.SemaphoreType.DMA((3,)),
        ],
        compiler_params=pltpu.CompilerParams(vmem_limit_bytes=16 * 1024 * 1024),
    )(*(pltpu.with_memory_space_constraint(a, pltpu.HBM) for a in (k, v, betas)))


def local_kernel(q_ref, k_ref, v_ref, g_ref, x_ref, e_ref, pre_ref, l_ref, m_ref, s_ref):
    heads = q_ref.shape[1] // HD
    blocks = q_ref.shape[0] // SPAN
    sub = 2 * SPAN
    seen = (order(lax.broadcasted_iota(jnp.int32, (SPAN, sub), 1)) >> 1) <= lax.broadcasted_iota(
        jnp.int32, (SPAN, sub), 0
    )
    spots = [
        (h * blocks + blk, slice(blk * SPAN, (blk + 1) * SPAN), slice(h * HD, (h + 1) * HD))
        for blk in range(blocks)
        for h in range(heads)
    ]
    num = range(len(spots))
    kb = [read_block(k_ref, i // heads, i % heads) for i in num]
    scores = [
        wide(jnp.where(seen, dot_nt(q_ref[rows, cols], kb[i]), 0.0) * e_ref[at, :1])
        for i, (at, rows, cols) in enumerate(spots)
    ]
    zq = [halves(dot(scores[i], square(x_ref[spots[i][0]]))) for i in num]
    carry = [
        (q_ref[rows, cols].astype(F32) - dot(wide(zq[i]), square(kb[i]))).astype(BF16)
        for i, (_, rows, cols) in enumerate(spots)
    ]
    loc = [
        dot(wide(zq[i] * e_ref[spots[i][0], 1:]), square(read_block(v_ref, i // heads, i % heads)))
        for i in num
    ]
    prod = [dot(carry[i], pre_ref[spots[i][0]]) for i in num]
    for i, (_, rows, cols) in enumerate(spots):
        qf = q_ref[rows, cols].astype(F32)
        unit = lax.rsqrt(jnp.sum(qf * qf, axis=1, keepdims=True) + 1e-6)
        m_ref[rows, cols] = (prod[i][:, :HD] * unit).astype(BF16)
        l_ref[rows, cols] = (loc[i] + prod[i][:, HD:]) * unit
        gate = g_ref[rows, cols].astype(F32)
        s_ref[rows, cols] = gate / (1.0 + jnp.exp(-gate))


def affine(a, b):
    return jnp.concatenate([a, b], axis=1)


def fold_kernel(x_ref, m_ref, send_ref, tot_ref, in_ref):
    peers, heads = m_ref.shape[:2]
    x = x_ref[0]
    r = lax.broadcasted_iota(jnp.int32, (HD, 2 * HD), 0)
    c = lax.broadcasted_iota(jnp.int32, (HD, 2 * HD), 1)
    zero = jnp.zeros((HD, HD), F32)
    total = [m_ref[0, h].astype(F32) for h in range(heads)]
    inside = [(r == c).astype(F32)] * heads
    for k in range(1, peers):
        for h in range(heads):
            inside[h] = jnp.where(x == k, total[h], inside[h])
            later = m_ref[k, h]
            prod = halves(dot(later[:, :HD], jnp.concatenate(split(total[h]), axis=1)))
            total[h] = prod + affine(zero, later[:, HD:].astype(F32))
    for h in range(heads):
        send_ref[h] = total[h].astype(BF16)
        tot_ref[h] = total[h]
        in_ref[h] = inside[h]


def join_kernel(later_ref, earlier_ref, send_ref, out_ref):
    zero = jnp.zeros((HD, HD), F32)
    for h in range(later_ref.shape[0]):
        later = later_ref[h]
        out = dot(wide(later[:, :HD]), square(earlier_ref[h])) + affine(zero, later[:, HD:])
        send_ref[h] = out.astype(BF16)
        out_ref[h] = out


def carry_kernel(later_ref, earlier_ref, send_ref):
    for h in range(later_ref.shape[0]):
        later = later_ref[h]
        state = dot(wide(later[:, :HD]), square(earlier_ref[h][:, HD:])) + later[:, HD:]
        send_ref[h] = state.astype(BF16)


def entry_kernel(in_ref, near_ref, far_ref, out_ref):
    zero = jnp.zeros((HD, HD), F32)
    for h in range(in_ref.shape[0]):
        near = near_ref[h]
        both = dot(near[:, :HD], far_ref[h]) + affine(zero, near[:, HD:].astype(F32))
        inner = in_ref[h]
        bh, bl = split(both)
        lhs = wide(inner[:, :HD])
        out = dot(lhs, square(bh)) + dot(lhs[:, :HD], bl)
        out_ref[h] = out + affine(zero, inner[:, HD:])


def mix_kernel(entry_ref, state_ref, l_ref, m_ref, s_ref, o_ref):
    for h in range(entry_ref.shape[0]):
        entry = entry_ref[h]
        start = dot(wide(entry[:, :HD]), square(state_ref[h])) + entry[:, HD:]
        cols = slice(h * HD, (h + 1) * HD)
        att = l_ref[:, cols] + dot(m_ref[:, cols], start.astype(BF16))
        scale = lax.rsqrt(jnp.mean(att * att, axis=1, keepdims=True) + 1e-6)
        o_ref[:, cols] = (att * scale * s_ref[:, cols]).astype(BF16)


VM = pl.BlockSpec(memory_space=pltpu.VMEM)
SM = pl.BlockSpec(memory_space=pltpu.SMEM)


def small(kernel, outs, *args, specs=None):
    return pl.pallas_call(
        kernel,
        out_shape=outs,
        in_specs=specs or [VM] * len(args),
        out_specs=jax.tree.map(lambda _: VM, outs),
        compiler_params=pltpu.CompilerParams(vmem_limit_bytes=16 * 1024 * 1024),
    )(*args)


def pack_kernel(chips, me_ref, w_ref, x_ref, ring_ref, sems):
    rows, width = w_ref.shape[0], ring_ref.shape[2]
    chip, core = me_ref[0] // 2, me_ref[0] % 2
    sign = 1 - 2 * (chip % 2)
    half = chips // 2
    hops = [half] + list(range(half - 1, 0, -1)) + list(range(1 - half, 0)) + [0]
    copies = []
    for i, hop in enumerate(hops):
        dest = (chip + chips + sign * hop) % chips
        block = pl.ds(pl.multiple_of((2 * dest + core) * width, width), width)
        for j, source in enumerate((w_ref, x_ref)):
            target = ring_ref.at[i, j * rows : (j + 1) * rows]
            copies.append(pltpu.make_async_copy(source.at[:, block], target, sems.at[2 * i + j]))
            copies[-1].start()
    for copy in copies:
        copy.wait()


def pack(chips, me, weight, mate_weight):
    rows = weight.shape[0]
    return pl.pallas_call(
        functools.partial(pack_kernel, chips),
        out_shape=jax.ShapeDtypeStruct((chips, 2 * rows, rows), BF16),
        in_specs=[SM] + [pl.BlockSpec(memory_space=pltpu.HBM)] * 2,
        out_specs=VM,
        scratch_shapes=[pltpu.SemaphoreType.DMA((2 * chips,))],
        compiler_params=pltpu.CompilerParams(vmem_limit_bytes=16 * 1024 * 1024),
    )(me, *(pltpu.with_memory_space_constraint(a, pltpu.HBM) for a in (weight, mate_weight)))


def term(a, b, w):
    rows = a.shape[1]
    return dot(a, w[:rows]) + dot(b, w[rows:])


def hop_kernel(jobs, got_count, me_ref, a_ref, b_ref, w_ref, *refs):
    odd = (me_ref[0] // 2) % 2
    got_refs, out_refs = refs[:got_count], refs[got_count:]
    cut = out_refs[0].shape[0]
    for i, (at, side) in enumerate(jobs):
        rows = pl.ds(pl.multiple_of(((odd + side) % 2) * cut, cut), cut)
        out = term(a_ref[rows, :], b_ref[rows, :], w_ref[at])
        if got_refs:
            out = out + got_refs[i][...].astype(F32)
        out_refs[i][...] = out.astype(BF16)


def own_kernel(me_ref, a_ref, b_ref, w_ref, even_ref, odd_ref, o_ref):
    odd = (me_ref[0] // 2) % 2
    cut = even_ref.shape[0]
    out = term(a_ref[...], b_ref[...], w_ref[w_ref.shape[0] - 1])
    for i in range(2):
        rows = slice(i * cut, (i + 1) * cut)
        got = jnp.where(odd == i, even_ref[...].astype(F32), odd_ref[...].astype(F32))
        o_ref[rows] = out[rows] + got


def last_kernel(me_ref, sum_ref, even_ref, odd_ref, o_ref):
    odd = (me_ref[0] // 2) % 2
    cut = even_ref.shape[0]
    for i in range(2):
        rows = slice(i * cut, (i + 1) * cut)
        got = jnp.where(odd == i, even_ref[...].astype(F32), odd_ref[...].astype(F32))
        o_ref[rows] = (sum_ref[rows] + got).astype(BF16)


def per_device(queries, keys, values, betas, gate, out_weight):
    tok, cols = queries.shape
    heads = cols // HD
    devices = lax.axis_size("head")
    chips = devices // 2
    me = lax.axis_index("head")
    core = me % 2

    def across(a, odd):
        pairs = [(c, (c + 1) % chips) for c in range(odd, chips, 2)]
        both = pairs + [(d, c) for c, d in pairs]
        return lax.ppermute(a, "head", [(2 * c + i, 2 * d + i) for c, d in both for i in range(2)])

    def mate(a):
        return lax.ppermute(a, "head", [(i, i ^ 1) for i in range(devices)])

    def later_z(a, by):
        groups = lax.axis_size("ctx_0")
        return lax.ppermute(a, "ctx_0", [(i, i + by) for i in range(groups - by)])

    mate_weight = mate(out_weight)
    maps, inverse, scales, prefixes = local_maps(keys, values, betas, 8)

    wide_map = jax.ShapeDtypeStruct((heads, HD, 2 * HD), F32)
    wide_send = jax.ShapeDtypeStruct((heads, HD, 2 * HD), BF16)
    state_send = jax.ShapeDtypeStruct((heads, HD, HD), BF16)
    gathered = lax.all_gather(maps, "ctx_1")
    x = lax.axis_index("ctx_1").astype(jnp.int32).reshape(1)
    send, total, inside = small(
        fold_kernel, (wide_send, wide_map, wide_map), x, gathered, specs=[SM, VM]
    )
    near = later_z(send, 1)
    send, pair = small(join_kernel, (wide_send, wide_map), total, near)
    far = later_z(send, 2)
    tokens = jax.ShapeDtypeStruct((tok, cols), F32)
    local, carry, silu = small(
        local_kernel,
        (tokens, jax.ShapeDtypeStruct((tok, cols), BF16), tokens),
        queries,
        keys,
        values,
        gate,
        inverse,
        scales,
        lax.optimization_barrier((prefixes, near))[0],
    )
    send = small(carry_kernel, state_send, pair, far)
    state = later_z(send, 4)
    entry = small(entry_kernel, wide_map, inside, near, far)
    place = me.astype(jnp.int32).reshape(1)
    ring_w = pack(chips, place, out_weight, lax.optimization_barrier((mate_weight, near))[0])
    entry = lax.optimization_barrier((entry, ring_w, silu))[0]
    mixed_in = small(
        mix_kernel,
        jax.ShapeDtypeStruct((tok, cols), BF16),
        entry,
        state,
        local,
        carry,
        silu,
    )
    mate_in = mate(mixed_in)

    half = chips // 2
    chunk = jax.ShapeDtypeStruct((tok // 2, cols), BF16)
    both = (mixed_in, mate_in, ring_w)

    def hop(jobs, prior, *got):
        got = [lax.optimization_barrier((g, prior))[0] for g in got]
        ins = both if prior is None or got else (lax.optimization_barrier((mixed_in, prior))[0], *both[1:])
        body = functools.partial(hop_kernel, jobs, len(got))
        return small(body, (chunk,) * len(jobs), place, *ins, *got, specs=[SM] + [VM] * (3 + len(got)))

    slots = [(half, 0)] + [s for k in range(half - 1, 0, -1) for s in ((k, 1), (k, 0))]
    prior, moved = None, []
    for n, (k, late) in enumerate(slots):
        at = [half - k, 0 if k == half else 2 * half - 1 - k]
        side = [late, 1 - late]
        if n < 2:
            ahead, back = hop([(at[0], side[0]), (at[1], side[1])], prior)
            prior = back
        else:
            from_even, from_odd = moved[n - 2]
            order = (1, 0) if n % 4 in (2, 3) else (0, 1)
            sums = {}
            for i in order:
                (sums[i],) = hop([(at[i], side[i])], prior, from_odd if i == 0 else from_even)
                prior = sums[i]
            ahead, back = sums[0], sums[1]
        moved.append((across(ahead, 0), across(back, 1)))
    (even_t, odd_t), (even_f, odd_f) = moved[-2:]
    total = small(
        own_kernel,
        jax.ShapeDtypeStruct((tok, cols), F32),
        place,
        *both,
        even_t,
        odd_t,
        specs=[SM] + [VM] * 5,
    )
    sent = jax.ShapeDtypeStruct((tok, cols), BF16)
    return small(last_kernel, sent, place, total, odd_f, even_f, specs=[SM] + [VM] * 3)


def solution(mesh):
    z = mesh.shape["ctx"] // 4
    finer = Mesh(mesh.devices.reshape(z, 4, mesh.shape["head"]), ("ctx_0", "ctx_1", "head"))
    in_specs = (
        P(CTX, "head"),
        P(None, CTX, "head"),
        P(None, CTX, "head"),
        P("head", None, CTX),
        P(CTX, "head"),
        P("head", None),
    )
    return jax.shard_map(
        per_device, mesh=finer, in_specs=in_specs, out_specs=P(CTX, "head"), check_vma=False
    )
```

```python
import functools
import jax
import jax.numpy as jnp
from jax import lax
from jax.experimental import pallas as pl
from jax.experimental.pallas import tpu as pltpu
from jax.sharding import Mesh
from jax.sharding import PartitionSpec as P

F32 = jnp.float32
BF16 = jnp.bfloat16
HD = 128
SPAN = 64
CTX = ("ctx_0", "ctx_1")


def dot(a, b):
    return jnp.dot(a, b, preferred_element_type=F32)


def dot_nt(a, b):
    return lax.dot_general(a, b, (((1,), (1,)), ((), ())), preferred_element_type=F32)


def split(x):
    hi = x.astype(BF16)
    return hi, (x - hi.astype(F32)).astype(BF16)


def wide(x):
    return jnp.concatenate(split(x), axis=1)


def square(pair):
    return jnp.concatenate([pair, pair], axis=0)


def halves(x):
    n = x.shape[1] // 2
    return x[:, :n] + x[:, n:]


def read_block(ref, blk, h):
    rows = [
        (j, pl.ds(pl.multiple_of(blk * SPAN + 16 * g, 16), 16))
        for g in range(SPAN // 16)
        for j in range(2)
    ]
    cols = slice(h * HD, (h + 1) * HD)
    return jnp.concatenate([ref[j, r, cols] for j, r in rows], axis=0)


def order(p):
    return (p & ~31) + 2 * (p & 15) + ((p >> 4) & 1)


def map_kernel(
    group, k_hbm, v_hbm, b_hbm, ab_ref, x_ref, e_ref, pre_ref, k_ref, v_ref, b_ref, lev_ref, p_ref, sems
):
    get_k = pltpu.make_async_copy(k_hbm, k_ref, sems.at[0])
    get_v = pltpu.make_async_copy(v_hbm, v_ref, sems.at[1])
    get_b = pltpu.make_async_copy(b_hbm, b_ref, sems.at[2])
    get_k.start()
    get_b.start()
    get_v.start()
    heads = k_ref.shape[2] // HD
    blocks = k_ref.shape[1] // SPAN
    sub = 2 * SPAN
    place_r = lax.broadcasted_iota(jnp.int32, (sub, sub), 0)
    place_c = lax.broadcasted_iota(jnp.int32, (sub, sub), 1)
    s_r, s_c = order(place_r), order(place_c)
    apart = s_r ^ s_c
    level = jnp.zeros((sub, sub), jnp.int32)
    for bit in range(1, 7):
        level = level + (apart >= 2**bit).astype(jnp.int32)
    lev_ref[...] = jnp.where(s_r > s_c, level, -1)
    eye = (place_r == place_c).astype(F32)
    for h in range(heads):
        p_ref[h] = jnp.concatenate([eye, jnp.zeros((HD, HD), F32)], axis=1)
    get_b.wait()
    get_k.wait()
    get_v.wait()

    for step in range(blocks // group):
        probs = [(step * group + i, h) for i in range(group) for h in range(heads)]
        kb = [read_block(k_ref, blk, h) for blk, h in probs]
        num = range(len(probs))
        n, e, N, X = [], [], [], []
        for i in num:
            blk, h = probs[i]
            gram = dot_nt(kb[i], kb[i])
            n2 = jnp.sum(gram * eye, axis=0, keepdims=True) + 1e-6
            first = blk * SPAN
            beta = jnp.concatenate(
                [
                    b_ref[h, j : j + 1, first + 16 * g : first + 16 * (g + 1)]
                    for g in range(SPAN // 16)
                    for j in range(2)
                ],
                axis=1,
            )
            e.append(beta / n2)
            n.append(jnp.sqrt(n2))
            e_ref[h * blocks + blk] = jnp.concatenate([e[i], n[i]], axis=0)
            N.append(jnp.where(lev_ref[...] >= 0, gram * e[i], 0.0))
            X.append(eye - jnp.where(lev_ref[...] == 0, N[i], 0.0))
        for lev in range(1, 7):
            xw = [wide(x) for x in X]
            Z = []
            for i in num:
                C = jnp.where(lev_ref[...] == lev, N[i], 0.0)
                Z.append(halves(dot(wide(C), square(xw[i]))))
            for i in num:
                X[i] = X[i] - halves(dot(xw[i], square(wide(Z[i]))))
        A, B = [], []
        for i in num:
            blk, h = probs[i]
            xw = wide(X[i])
            x_ref[h * blocks + blk] = xw
            ke = wide(kb[i].T.astype(F32) * e[i])
            y = halves(dot(ke, square(xw)))
            A.append(wide(eye - dot(wide(y), square(kb[i]))))
            B.append(dot(wide(y * n[i]), square(read_block(v_ref, blk, h))))
        for i in num:
            blk, h = probs[i]
            p = p_ref[h]
            ph, plo = split(p)
            pre_ref[h * blocks + blk] = ph
            new = dot(A[i], square(ph)) + dot(A[i][:, :HD], plo)
            p_ref[h] = new + jnp.concatenate([jnp.zeros((HD, HD), F32), B[i]], axis=1)
    for h in range(heads):
        ab_ref[h] = p_ref[h].astype(BF16)


def local_maps(k, v, betas, group):
    _, tok, cols = k.shape
    heads = cols // HD
    count = heads * tok // SPAN
    return pl.pallas_call(
        functools.partial(map_kernel, group),
        out_shape=(
            jax.ShapeDtypeStruct((heads, HD, 2 * HD), BF16),
            jax.ShapeDtypeStruct((count, 2 * SPAN, 4 * SPAN), BF16),
            jax.ShapeDtypeStruct((count, 2, 2 * SPAN), F32),
            jax.ShapeDtypeStruct((count, HD, 2 * HD), BF16),
        ),
        in_specs=[pl.BlockSpec(memory_space=pltpu.HBM)] * 3,
        out_specs=[pl.BlockSpec(memory_space=pltpu.VMEM)] * 4,
        scratch_shapes=[
            pltpu.VMEM(k.shape, k.dtype),
            pltpu.VMEM(v.shape, v.dtype),
            pltpu.VMEM(betas.shape, betas.dtype),
            pltpu.VMEM((2 * SPAN, 2 * SPAN), jnp.int32),
            pltpu.VMEM((heads, HD, 2 * HD), F32),
            pltpu.SemaphoreType.DMA((3,)),
        ],
        compiler_params=pltpu.CompilerParams(vmem_limit_bytes=16 * 1024 * 1024),
    )(*(pltpu.with_memory_space_constraint(a, pltpu.HBM) for a in (k, v, betas)))


def local_kernel(q_ref, k_ref, v_ref, g_ref, x_ref, e_ref, pre_ref, l_ref, m_ref, s_ref):
    heads = q_ref.shape[1] // HD
    blocks = q_ref.shape[0] // SPAN
    sub = 2 * SPAN
    seen = (order(lax.broadcasted_iota(jnp.int32, (SPAN, sub), 1)) >> 1) <= lax.broadcasted_iota(
        jnp.int32, (SPAN, sub), 0
    )
    spots = [
        (h * blocks + blk, slice(blk * SPAN, (blk + 1) * SPAN), slice(h * HD, (h + 1) * HD))
        for blk in range(blocks)
        for h in range(heads)
    ]
    num = range(len(spots))
    kb = [read_block(k_ref, i // heads, i % heads) for i in num]
    scores = [
        wide(jnp.where(seen, dot_nt(q_ref[rows, cols], kb[i]), 0.0) * e_ref[at, :1])
        for i, (at, rows, cols) in enumerate(spots)
    ]
    zq = [halves(dot(scores[i], square(x_ref[spots[i][0]]))) for i in num]
    carry = [
        (q_ref[rows, cols].astype(F32) - dot(wide(zq[i]), square(kb[i]))).astype(BF16)
        for i, (_, rows, cols) in enumerate(spots)
    ]
    loc = [
        dot(wide(zq[i] * e_ref[spots[i][0], 1:]), square(read_block(v_ref, i // heads, i % heads)))
        for i in num
    ]
    prod = [dot(carry[i], pre_ref[spots[i][0]]) for i in num]
    for i, (_, rows, cols) in enumerate(spots):
        qf = q_ref[rows, cols].astype(F32)
        unit = lax.rsqrt(jnp.sum(qf * qf, axis=1, keepdims=True) + 1e-6)
        m_ref[rows, cols] = (prod[i][:, :HD] * unit).astype(BF16)
        l_ref[rows, cols] = (loc[i] + prod[i][:, HD:]) * unit
        gate = g_ref[rows, cols].astype(F32)
        s_ref[rows, cols] = gate / (1.0 + jnp.exp(-gate))


def affine(a, b):
    return jnp.concatenate([a, b], axis=1)


def fold_kernel(x_ref, m_ref, send_ref, tot_ref, in_ref):
    peers, heads = m_ref.shape[:2]
    x = x_ref[0]
    r = lax.broadcasted_iota(jnp.int32, (HD, 2 * HD), 0)
    c = lax.broadcasted_iota(jnp.int32, (HD, 2 * HD), 1)
    zero = jnp.zeros((HD, HD), F32)
    total = [m_ref[0, h].astype(F32) for h in range(heads)]
    inside = [(r == c).astype(F32)] * heads
    for k in range(1, peers):
        for h in range(heads):
            inside[h] = jnp.where(x == k, total[h], inside[h])
            later = m_ref[k, h]
            prod = halves(dot(later[:, :HD], jnp.concatenate(split(total[h]), axis=1)))
            total[h] = prod + affine(zero, later[:, HD:].astype(F32))
    for h in range(heads):
        send_ref[h] = total[h].astype(BF16)
        tot_ref[h] = total[h]
        in_ref[h] = inside[h]


def join_kernel(later_ref, earlier_ref, send_ref, out_ref):
    zero = jnp.zeros((HD, HD), F32)
    for h in range(later_ref.shape[0]):
        later = later_ref[h]
        out = dot(wide(later[:, :HD]), square(earlier_ref[h])) + affine(zero, later[:, HD:])
        send_ref[h] = out.astype(BF16)
        out_ref[h] = out


def carry_kernel(later_ref, earlier_ref, send_ref):
    for h in range(later_ref.shape[0]):
        later = later_ref[h]
        state = dot(wide(later[:, :HD]), square(earlier_ref[h][:, HD:])) + later[:, HD:]
        send_ref[h] = state.astype(BF16)


def entry_kernel(in_ref, near_ref, far_ref, out_ref):
    zero = jnp.zeros((HD, HD), F32)
    for h in range(in_ref.shape[0]):
        near = near_ref[h]
        both = dot(near[:, :HD], far_ref[h]) + affine(zero, near[:, HD:].astype(F32))
        inner = in_ref[h]
        bh, bl = split(both)
        lhs = wide(inner[:, :HD])
        out = dot(lhs, square(bh)) + dot(lhs[:, :HD], bl)
        out_ref[h] = out + affine(zero, inner[:, HD:])


def mix_kernel(entry_ref, state_ref, l_ref, m_ref, s_ref, o_ref):
    for h in range(entry_ref.shape[0]):
        entry = entry_ref[h]
        start = dot(wide(entry[:, :HD]), square(state_ref[h])) + entry[:, HD:]
        cols = slice(h * HD, (h + 1) * HD)
        att = l_ref[:, cols] + dot(m_ref[:, cols], start.astype(BF16))
        scale = lax.rsqrt(jnp.mean(att * att, axis=1, keepdims=True) + 1e-6)
        o_ref[:, cols] = (att * scale * s_ref[:, cols]).astype(BF16)


VM = pl.BlockSpec(memory_space=pltpu.VMEM)
SM = pl.BlockSpec(memory_space=pltpu.SMEM)


def small(kernel, outs, *args, specs=None):
    return pl.pallas_call(
        kernel,
        out_shape=outs,
        in_specs=specs or [VM] * len(args),
        out_specs=jax.tree.map(lambda _: VM, outs),
        compiler_params=pltpu.CompilerParams(vmem_limit_bytes=16 * 1024 * 1024),
    )(*args)


def pack_kernel(chips, me_ref, w_ref, x_ref, ring_ref, sems):
    rows, width = w_ref.shape[0], ring_ref.shape[2]
    chip, core = me_ref[0] // 2, me_ref[0] % 2
    sign = 1 - 2 * (chip % 2)
    half = chips // 2
    hops = [half] + list(range(half - 1, 0, -1)) + list(range(1 - half, 0)) + [0]
    copies = []
    for i, hop in enumerate(hops):
        dest = (chip + chips + sign * hop) % chips
        block = pl.ds(pl.multiple_of((2 * dest + core) * width, width), width)
        for j, source in enumerate((w_ref, x_ref)):
            target = ring_ref.at[i, j * rows : (j + 1) * rows]
            copies.append(pltpu.make_async_copy(source.at[:, block], target, sems.at[2 * i + j]))
            copies[-1].start()
    for copy in copies:
        copy.wait()


def pack(chips, me, weight, mate_weight):
    rows = weight.shape[0]
    return pl.pallas_call(
        functools.partial(pack_kernel, chips),
        out_shape=jax.ShapeDtypeStruct((chips, 2 * rows, rows), BF16),
        in_specs=[SM] + [pl.BlockSpec(memory_space=pltpu.HBM)] * 2,
        out_specs=VM,
        scratch_shapes=[pltpu.SemaphoreType.DMA((2 * chips,))],
        compiler_params=pltpu.CompilerParams(vmem_limit_bytes=16 * 1024 * 1024),
    )(me, *(pltpu.with_memory_space_constraint(a, pltpu.HBM) for a in (weight, mate_weight)))


def term(a, b, w):
    rows = a.shape[1]
    return dot(a, w[:rows]) + dot(b, w[rows:])


def far_kernel(me_ref, a_ref, b_ref, w_ref, ahead_ref, back_ref):
    odd = (me_ref[0] // 2) % 2 != 0
    out = term(a_ref[...], b_ref[...], w_ref[0]).astype(BF16)
    cut = ahead_ref.shape[0]
    ahead_ref[...] = jnp.where(odd, out[cut:], out[:cut])
    back_ref[...] = jnp.where(odd, out[:cut], out[cut:])


def hop_kernel(at, side, me_ref, a_ref, b_ref, w_ref, got_ref, o_ref):
    odd = (me_ref[0] // 2) % 2
    out = term(a_ref[...], b_ref[...], w_ref[at])
    cut = got_ref.shape[0]
    for i in range(2):
        rows = slice(i * cut, (i + 1) * cut)
        got = jnp.where((odd + side) % 2 == i, got_ref[...].astype(F32), 0.0)
        o_ref[rows] = (out[rows] + got).astype(BF16)


def rest_kernel(picks, a_ref, b_ref, w_ref, o_ref):
    for i, at in enumerate(picks):
        o_ref[i] = term(a_ref[...], b_ref[...], w_ref[at])


def add_kernel(at, terms_ref, got_ref, o_ref):
    o_ref[...] = (terms_ref[at] + got_ref[...].astype(F32)).astype(o_ref.dtype)


def last_kernel(sum_ref, got_ref, o_ref):
    o_ref[...] = (sum_ref[...] + got_ref[...].astype(F32)).astype(BF16)


def per_device(queries, keys, values, betas, gate, out_weight):
    tok, cols = queries.shape
    heads = cols // HD
    devices = lax.axis_size("head")
    chips = devices // 2
    me = lax.axis_index("head")
    core = me % 2

    def across(a, odd):
        pairs = [(c, (c + 1) % chips) for c in range(odd, chips, 2)]
        both = pairs + [(d, c) for c, d in pairs]
        return lax.ppermute(a, "head", [(2 * c + i, 2 * d + i) for c, d in both for i in range(2)])

    def mate(a):
        return lax.ppermute(a, "head", [(i, i ^ 1) for i in range(devices)])

    def later_z(a, by):
        groups = lax.axis_size("ctx_0")
        return lax.ppermute(a, "ctx_0", [(i, i + by) for i in range(groups - by)])

    mate_weight = mate(out_weight)
    maps, inverse, scales, prefixes = local_maps(keys, values, betas, 8)

    wide_map = jax.ShapeDtypeStruct((heads, HD, 2 * HD), F32)
    wide_send = jax.ShapeDtypeStruct((heads, HD, 2 * HD), BF16)
    state_send = jax.ShapeDtypeStruct((heads, HD, HD), BF16)
    tokens = jax.ShapeDtypeStruct((tok, cols), F32)
    gathered = lax.all_gather(maps, "ctx_1")
    x = lax.axis_index("ctx_1").astype(jnp.int32).reshape(1)
    send, total, inside = small(
        fold_kernel, (wide_send, wide_map, wide_map), x, gathered, specs=[SM, VM]
    )
    near = later_z(send, 1)
    local, carry, silu = small(
        local_kernel,
        (tokens, jax.ShapeDtypeStruct((tok, cols), BF16), tokens),
        queries,
        keys,
        values,
        gate,
        inverse,
        scales,
        lax.optimization_barrier((prefixes, total))[0],
    )
    near = lax.optimization_barrier((near, silu))[0]
    send, pair = small(join_kernel, (wide_send, wide_map), total, near)
    far = later_z(send, 2)
    place = me.astype(jnp.int32).reshape(1)
    ring_w = pack(chips, place, out_weight, lax.optimization_barrier((mate_weight, pair))[0])
    far = lax.optimization_barrier((far, ring_w))[0]
    send = small(carry_kernel, state_send, pair, far)
    state = later_z(send, 4)
    entry = small(entry_kernel, wide_map, inside, near, far)
    mixed_in = small(
        mix_kernel,
        jax.ShapeDtypeStruct((tok, cols), BF16),
        entry,
        state,
        local,
        carry,
        silu,
    )
    mate_in = mate(mixed_in)

    half = chips // 2
    sent = jax.ShapeDtypeStruct((tok, cols), BF16)
    part = jax.ShapeDtypeStruct((tok // 2, cols), BF16)
    both = (mixed_in, mate_in, ring_w)
    ahead, back = small(far_kernel, (part, part), place, *both, specs=[SM] + [VM] * 3)
    got, prior, terms = (across(back, 1), across(ahead, 0)), None, None
    for k in range(half - 1, 0, -1):
        sums = [None, None]
        for i in (1, 0) if k % 2 else (0, 1):
            came = got[i]
            if prior is not None:
                came = lax.optimization_barrier((came, prior))[0]
            if k == half - 1:
                body = functools.partial(hop_kernel, 1 + i * (half - 1), i)
                sums[i] = small(body, sent, place, *both, came, specs=[SM] + [VM] * 4)
            else:
                body = functools.partial(add_kernel, 2 * (half - 2 - k) + i)
                sums[i] = small(body, sent, terms, came)
            prior = sums[i]
        if k == half - 1:
            picks = [j + i * (half - 1) for j in range(2, half) for i in range(2)] + [chips - 1]
            terms = small(
                functools.partial(rest_kernel, picks),
                jax.ShapeDtypeStruct((len(picks), tok, cols), F32),
                lax.optimization_barrier((mixed_in, prior))[0],
                mate_in,
                ring_w,
            )
        got = (across(sums[1], 1), across(sums[0], 0))
    came = lax.optimization_barrier((got[0], prior))[0]
    total = small(functools.partial(add_kernel, 2 * half - 4), tokens, terms, came)
    return small(last_kernel, sent, total, got[1])


def solution(mesh):
    z = mesh.shape["ctx"] // 4
    finer = Mesh(mesh.devices.reshape(z, 4, mesh.shape["head"]), ("ctx_0", "ctx_1", "head"))
    in_specs = (
        P(CTX, "head"),
        P(None, CTX, "head"),
        P(None, CTX, "head"),
        P("head", None, CTX),
        P(CTX, "head"),
        P("head", None),
    )
    return jax.shard_map(
        per_device, mesh=finer, in_specs=in_specs, out_specs=P(CTX, "head"), check_vma=False
    )
```

```python
import functools
import jax
import jax.numpy as jnp
from jax import lax
from jax.experimental import pallas as pl
from jax.experimental.pallas import tpu as pltpu
from jax.sharding import Mesh
from jax.sharding import PartitionSpec as P

F32 = jnp.float32
BF16 = jnp.bfloat16
HD = 128
SPAN = 64
CTX = ("ctx_0", "ctx_1")


def dot(a, b):
    return jnp.dot(a, b, preferred_element_type=F32)


def dot_nt(a, b):
    return lax.dot_general(a, b, (((1,), (1,)), ((), ())), preferred_element_type=F32)


def split(x):
    hi = x.astype(BF16)
    return hi, (x - hi.astype(F32)).astype(BF16)


def wide(x):
    return jnp.concatenate(split(x), axis=1)


def square(pair):
    return jnp.concatenate([pair, pair], axis=0)


def halves(x):
    n = x.shape[1] // 2
    return x[:, :n] + x[:, n:]


def read_block(ref, blk, h):
    rows = [
        (j, pl.ds(pl.multiple_of(blk * SPAN + 16 * g, 16), 16))
        for g in range(SPAN // 16)
        for j in range(2)
    ]
    cols = slice(h * HD, (h + 1) * HD)
    return jnp.concatenate([ref[j, r, cols] for j, r in rows], axis=0)


def order(p):
    return (p & ~31) + 2 * (p & 15) + ((p >> 4) & 1)


def map_kernel(
    group, k_hbm, v_hbm, b_hbm, ab_ref, x_ref, e_ref, a_ref, c_ref, k_ref, v_ref, b_ref, lev_ref, sems
):
    copies = [pltpu.make_async_copy(b_hbm, b_ref, sems.at[0])]
    piece = k_ref.shape[1] // 4
    for source, target in ((k_hbm, k_ref), (v_hbm, v_ref)):
        for j in range(2):
            for i in range(4):
                part = (j, slice(i * piece, (i + 1) * piece))
                at = sems.at[len(copies)]
                copies.append(pltpu.make_async_copy(source.at[part], target.at[part], at))
    for copy in copies:
        copy.start()
    heads = k_ref.shape[2] // HD
    blocks = k_ref.shape[1] // SPAN
    sub = 2 * SPAN
    place_r = lax.broadcasted_iota(jnp.int32, (sub, sub), 0)
    place_c = lax.broadcasted_iota(jnp.int32, (sub, sub), 1)
    s_r, s_c = order(place_r), order(place_c)
    apart = s_r ^ s_c
    level = jnp.zeros((sub, sub), jnp.int32)
    for bit in range(1, 7):
        level = level + (apart >= 2**bit).astype(jnp.int32)
    lev_ref[...] = jnp.where(s_r > s_c, level, -1)
    eye = (place_r == place_c).astype(F32)
    for copy in copies:
        copy.wait()

    blocks_of = [[] for _ in range(heads)]
    for step in range(blocks // group):
        probs = [(step * group + i, h) for i in range(group) for h in range(heads)]
        kb = [read_block(k_ref, blk, h) for blk, h in probs]
        num = range(len(probs))
        n, e, N, X = [], [], [], []
        for i in num:
            blk, h = probs[i]
            gram = dot_nt(kb[i], kb[i])
            n2 = jnp.sum(gram * eye, axis=0, keepdims=True) + 1e-6
            first = blk * SPAN
            beta = jnp.concatenate(
                [
                    b_ref[h, j : j + 1, first + 16 * g : first + 16 * (g + 1)]
                    for g in range(SPAN // 16)
                    for j in range(2)
                ],
                axis=1,
            )
            e.append(beta / n2)
            n.append(jnp.sqrt(n2))
            e_ref[h * blocks + blk] = jnp.concatenate([e[i], n[i]], axis=0)
            N.append(jnp.where(lev_ref[...] >= 0, gram * e[i], 0.0))
            X.append(eye - jnp.where(lev_ref[...] == 0, N[i], 0.0))
        for lev in range(1, 7):
            xw = [wide(x) for x in X]
            Z = []
            for i in num:
                C = jnp.where(lev_ref[...] == lev, N[i], 0.0)
                Z.append(halves(dot(wide(C), square(xw[i]))))
            for i in num:
                X[i] = X[i] - halves(dot(xw[i], square(wide(Z[i]))))
        A, B = [], []
        for i in num:
            blk, h = probs[i]
            xw = wide(X[i])
            x_ref[h * blocks + blk] = xw
            ke = wide(kb[i].T.astype(F32) * e[i])
            y = halves(dot(ke, square(xw)))
            A.append(wide(eye - dot(wide(y), square(kb[i]))))
            B.append(dot(wide(y * n[i]), square(read_block(v_ref, blk, h))))
        for i in num:
            blk, h = probs[i]
            a_ref[h * blocks + blk] = A[i]
            c_ref[h * blocks + blk] = B[i]
            blocks_of[h].append((A[i], B[i]))

    while len(blocks_of[0]) > 1:
        blocks_of = [
            [joined(maps[i + 1], maps[i]) for i in range(0, len(maps), 2)] for maps in blocks_of
        ]
    for h in range(heads):
        a, c = blocks_of[h][0]
        ab_ref[h] = jnp.concatenate([a[:, :HD], c.astype(BF16)], axis=1)


def joined(later, earlier):
    left, source = later
    b_hi, b_lo = split(earlier[1])
    hi = jnp.concatenate([earlier[0][:, :HD], b_hi], axis=1)
    lo = jnp.concatenate([earlier[0][:, HD:], b_lo], axis=1)
    new = dot(left, square(hi)) + dot(left[:, :HD], lo)
    return wide(new[:, :HD]), new[:, HD:] + source


def local_maps(k, v, betas, group):
    _, tok, cols = k.shape
    heads = cols // HD
    count = heads * tok // SPAN
    return pl.pallas_call(
        functools.partial(map_kernel, group),
        out_shape=(
            jax.ShapeDtypeStruct((heads, HD, 2 * HD), BF16),
            jax.ShapeDtypeStruct((count, 2 * SPAN, 4 * SPAN), BF16),
            jax.ShapeDtypeStruct((count, 2, 2 * SPAN), F32),
            jax.ShapeDtypeStruct((count, HD, 2 * HD), BF16),
            jax.ShapeDtypeStruct((count, HD, HD), F32),
        ),
        in_specs=[pl.BlockSpec(memory_space=pltpu.HBM)] * 3,
        out_specs=[pl.BlockSpec(memory_space=pltpu.VMEM)] * 5,
        scratch_shapes=[
            pltpu.VMEM(k.shape, k.dtype),
            pltpu.VMEM(v.shape, v.dtype),
            pltpu.VMEM(betas.shape, betas.dtype),
            pltpu.VMEM((2 * SPAN, 2 * SPAN), jnp.int32),
            pltpu.SemaphoreType.DMA((17,)),
        ],
        compiler_params=pltpu.CompilerParams(vmem_limit_bytes=16 * 1024 * 1024),
    )(*(pltpu.with_memory_space_constraint(a, pltpu.HBM) for a in (k, v, betas)))


def local_kernel(q_ref, k_ref, v_ref, g_ref, x_ref, e_ref, a_ref, c_ref, l_ref, m_ref, s_ref):
    heads = q_ref.shape[1] // HD
    blocks = q_ref.shape[0] // SPAN
    sub = 2 * SPAN
    seen = (order(lax.broadcasted_iota(jnp.int32, (SPAN, sub), 1)) >> 1) <= lax.broadcasted_iota(
        jnp.int32, (SPAN, sub), 0
    )
    spots = [
        (h * blocks + blk, slice(blk * SPAN, (blk + 1) * SPAN), slice(h * HD, (h + 1) * HD))
        for blk in range(blocks)
        for h in range(heads)
    ]
    num = range(len(spots))
    kb = [read_block(k_ref, i // heads, i % heads) for i in num]
    scores = [
        wide(jnp.where(seen, dot_nt(q_ref[rows, cols], kb[i]), 0.0) * e_ref[at, :1])
        for i, (at, rows, cols) in enumerate(spots)
    ]
    zq = [halves(dot(scores[i], square(x_ref[spots[i][0]]))) for i in num]
    carry = [
        (q_ref[rows, cols].astype(F32) - dot(wide(zq[i]), square(kb[i]))).astype(BF16)
        for i, (_, rows, cols) in enumerate(spots)
    ]
    loc = [
        dot(wide(zq[i] * e_ref[spots[i][0], 1:]), square(read_block(v_ref, i // heads, i % heads)))
        for i in num
    ]
    prefix = {}
    r = lax.broadcasted_iota(jnp.int32, (HD, 2 * HD), 0)
    c = lax.broadcasted_iota(jnp.int32, (HD, 2 * HD), 1)
    state = [(r == c).astype(F32)] * heads
    for i in num:
        at, h = spots[i][0], i % heads
        hi, lo = split(state[h])
        prefix[i] = hi
        if i < len(spots) - heads:
            left = a_ref[at]
            new = dot(left, square(hi)) + dot(left[:, :HD], lo)
            state[h] = jnp.concatenate([new[:, :HD], new[:, HD:] + c_ref[at]], axis=1)
    prod = [dot(carry[i], prefix[i]) for i in num]
    for i, (_, rows, cols) in enumerate(spots):
        qf = q_ref[rows, cols].astype(F32)
        unit = lax.rsqrt(jnp.sum(qf * qf, axis=1, keepdims=True) + 1e-6)
        m_ref[rows, cols] = (prod[i][:, :HD] * unit).astype(BF16)
        l_ref[rows, cols] = (loc[i] + prod[i][:, HD:]) * unit
        gate = g_ref[rows, cols].astype(F32)
        s_ref[rows, cols] = gate / (1.0 + jnp.exp(-gate))


def affine(a, b):
    return jnp.concatenate([a, b], axis=1)


def fold_kernel(x_ref, m_ref, send_ref, tot_ref, in_ref):
    peers, heads = m_ref.shape[:2]
    x = x_ref[0]
    r = lax.broadcasted_iota(jnp.int32, (HD, 2 * HD), 0)
    c = lax.broadcasted_iota(jnp.int32, (HD, 2 * HD), 1)
    zero = jnp.zeros((HD, HD), F32)
    total = [m_ref[0, h].astype(F32) for h in range(heads)]
    inside = [(r == c).astype(F32)] * heads
    for k in range(1, peers):
        for h in range(heads):
            inside[h] = jnp.where(x == k, total[h], inside[h])
            later = m_ref[k, h]
            prod = halves(dot(later[:, :HD], jnp.concatenate(split(total[h]), axis=1)))
            total[h] = prod + affine(zero, later[:, HD:].astype(F32))
    for h in range(heads):
        send_ref[h] = total[h].astype(BF16)
        tot_ref[h] = total[h]
        in_ref[h] = inside[h]


def join_kernel(later_ref, earlier_ref, send_ref, out_ref):
    zero = jnp.zeros((HD, HD), F32)
    for h in range(later_ref.shape[0]):
        later = later_ref[h]
        out = dot(wide(later[:, :HD]), square(earlier_ref[h])) + affine(zero, later[:, HD:])
        send_ref[h] = out.astype(BF16)
        out_ref[h] = out


def carry_kernel(later_ref, earlier_ref, send_ref):
    for h in range(later_ref.shape[0]):
        later = later_ref[h]
        state = dot(wide(later[:, :HD]), square(earlier_ref[h][:, HD:])) + later[:, HD:]
        send_ref[h] = state.astype(BF16)


def entry_kernel(in_ref, near_ref, far_ref, out_ref):
    zero = jnp.zeros((HD, HD), F32)
    for h in range(in_ref.shape[0]):
        near = near_ref[h]
        both = dot(near[:, :HD], far_ref[h]) + affine(zero, near[:, HD:].astype(F32))
        inner = in_ref[h]
        bh, bl = split(both)
        lhs = wide(inner[:, :HD])
        out = dot(lhs, square(bh)) + dot(lhs[:, :HD], bl)
        out_ref[h] = out + affine(zero, inner[:, HD:])


def mix_kernel(entry_ref, state_ref, l_ref, m_ref, s_ref, o_ref):
    for h in range(entry_ref.shape[0]):
        entry = entry_ref[h]
        start = dot(wide(entry[:, :HD]), square(state_ref[h])) + entry[:, HD:]
        cols = slice(h * HD, (h + 1) * HD)
        att = l_ref[:, cols] + dot(m_ref[:, cols], start.astype(BF16))
        scale = lax.rsqrt(jnp.mean(att * att, axis=1, keepdims=True) + 1e-6)
        o_ref[:, cols] = (att * scale * s_ref[:, cols]).astype(BF16)


VM = pl.BlockSpec(memory_space=pltpu.VMEM)
SM = pl.BlockSpec(memory_space=pltpu.SMEM)


def small(kernel, outs, *args, specs=None):
    return pl.pallas_call(
        kernel,
        out_shape=outs,
        in_specs=specs or [VM] * len(args),
        out_specs=jax.tree.map(lambda _: VM, outs),
        compiler_params=pltpu.CompilerParams(vmem_limit_bytes=16 * 1024 * 1024),
    )(*args)


def pack_kernel(chips, me_ref, w_ref, x_ref, ring_ref, sems):
    rows, width = w_ref.shape[0], ring_ref.shape[2]
    chip, core = me_ref[0] // 2, me_ref[0] % 2
    sign = 1 - 2 * (chip % 2)
    half = chips // 2
    hops = [half] + list(range(half - 1, 0, -1)) + list(range(1 - half, 0)) + [0]
    copies = []
    for i, hop in enumerate(hops):
        dest = (chip + chips + sign * hop) % chips
        block = pl.ds(pl.multiple_of((2 * dest + core) * width, width), width)
        for j, source in enumerate((w_ref, x_ref)):
            target = ring_ref.at[i, j * rows : (j + 1) * rows]
            copies.append(pltpu.make_async_copy(source.at[:, block], target, sems.at[2 * i + j]))
            copies[-1].start()
    for copy in copies:
        copy.wait()


def pack(chips, me, weight, mate_weight):
    rows = weight.shape[0]
    return pl.pallas_call(
        functools.partial(pack_kernel, chips),
        out_shape=jax.ShapeDtypeStruct((chips, 2 * rows, rows), BF16),
        in_specs=[SM] + [pl.BlockSpec(memory_space=pltpu.HBM)] * 2,
        out_specs=VM,
        scratch_shapes=[pltpu.SemaphoreType.DMA((2 * chips,))],
        compiler_params=pltpu.CompilerParams(vmem_limit_bytes=16 * 1024 * 1024),
    )(me, *(pltpu.with_memory_space_constraint(a, pltpu.HBM) for a in (weight, mate_weight)))


def term(a, b, w):
    rows = a.shape[1]
    return dot(a, w[:rows]) + dot(b, w[rows:])


def term_kernel(at, a_ref, b_ref, w_ref, o_ref):
    o_ref[...] = term(a_ref[...], b_ref[...], w_ref[at]).astype(BF16)


def hop_kernel(at, a_ref, b_ref, w_ref, got_ref, o_ref):
    out = term(a_ref[...], b_ref[...], w_ref[at])
    o_ref[...] = (out + got_ref[...].astype(F32)).astype(BF16)


def rest_kernel(picks, a_ref, b_ref, w_ref, o_ref):
    for i, at in enumerate(picks):
        o_ref[i] = term(a_ref[...], b_ref[...], w_ref[at])


def add_kernel(at, terms_ref, got_ref, o_ref):
    o_ref[...] = (terms_ref[at] + got_ref[...].astype(F32)).astype(o_ref.dtype)


def last_kernel(sum_ref, got_ref, o_ref):
    o_ref[...] = (sum_ref[...] + got_ref[...].astype(F32)).astype(BF16)


def per_device(queries, keys, values, betas, gate, out_weight):
    tok, cols = queries.shape
    heads = cols // HD
    devices = lax.axis_size("head")
    chips = devices // 2
    me = lax.axis_index("head")
    core = me % 2

    def across(a, odd):
        pairs = [(c, (c + 1) % chips) for c in range(odd, chips, 2)]
        both = pairs + [(d, c) for c, d in pairs]
        return lax.ppermute(a, "head", [(2 * c + i, 2 * d + i) for c, d in both for i in range(2)])

    def mate(a):
        return lax.ppermute(a, "head", [(i, i ^ 1) for i in range(devices)])

    def later_z(a, by):
        groups = lax.axis_size("ctx_0")
        return lax.ppermute(a, "ctx_0", [(i, i + by) for i in range(groups - by)])

    mate_weight = mate(out_weight)
    maps, inverse, scales, lefts, sources = local_maps(keys, values, betas, 8)

    wide_map = jax.ShapeDtypeStruct((heads, HD, 2 * HD), F32)
    wide_send = jax.ShapeDtypeStruct((heads, HD, 2 * HD), BF16)
    state_send = jax.ShapeDtypeStruct((heads, HD, HD), BF16)
    tokens = jax.ShapeDtypeStruct((tok, cols), F32)
    gathered = lax.all_gather(maps, "ctx_1")
    x = lax.axis_index("ctx_1").astype(jnp.int32).reshape(1)
    send, total, inside = small(
        fold_kernel, (wide_send, wide_map, wide_map), x, gathered, specs=[SM, VM]
    )
    near = later_z(send, 1)
    local, carry, silu = small(
        local_kernel,
        (tokens, jax.ShapeDtypeStruct((tok, cols), BF16), tokens),
        queries,
        keys,
        values,
        gate,
        inverse,
        scales,
        lax.optimization_barrier((lefts, total))[0],
        sources,
    )
    near = lax.optimization_barrier((near, silu))[0]
    send, pair = small(join_kernel, (wide_send, wide_map), total, near)
    far = later_z(send, 2)
    place = me.astype(jnp.int32).reshape(1)
    ring_w = pack(chips, place, out_weight, lax.optimization_barrier((mate_weight, pair))[0])
    far = lax.optimization_barrier((far, ring_w))[0]
    send = small(carry_kernel, state_send, pair, far)
    state = later_z(send, 4)
    entry = small(entry_kernel, wide_map, inside, near, far)
    mixed_in = small(
        mix_kernel,
        jax.ShapeDtypeStruct((tok, cols), BF16),
        entry,
        state,
        local,
        carry,
        silu,
    )
    mate_in = mate(mixed_in)

    half = chips // 2
    sent = jax.ShapeDtypeStruct((tok, cols), BF16)
    both = (mixed_in, mate_in, ring_w)
    far = small(functools.partial(term_kernel, 0), sent, *both)
    came = across(far, 0)
    late_in = lax.optimization_barrier((mixed_in, far))[0]
    third = small(functools.partial(term_kernel, 1), sent, late_in, mate_in, ring_w)
    came = lax.optimization_barrier((came, third))[0]
    prior = small(functools.partial(hop_kernel, half), sent, *both, came)
    got = (across(prior, 1), across(third, 0))
    picks = [j + i * (half - 1) for j in range(2, half) for i in range(2)] + [chips - 1]
    terms = small(
        functools.partial(rest_kernel, picks),
        jax.ShapeDtypeStruct((len(picks), tok, cols), F32),
        lax.optimization_barrier((mixed_in, prior))[0],
        mate_in,
        ring_w,
    )
    for k in range(half - 2, 0, -1):
        sums = [None, None]
        for i in (0, 1) if k % 2 else (1, 0):
            came = lax.optimization_barrier((got[i], prior))[0]
            body = functools.partial(add_kernel, 2 * (half - 2 - k) + i)
            sums[i] = prior = small(body, sent, terms, came)
        got = (across(sums[1], 1), across(sums[0], 0))
    came = lax.optimization_barrier((got[1], prior))[0]
    total = small(functools.partial(add_kernel, 2 * half - 4), tokens, terms, came)
    return small(last_kernel, sent, total, got[0])


def solution(mesh):
    z = mesh.shape["ctx"] // 4
    finer = Mesh(mesh.devices.reshape(z, 4, mesh.shape["head"]), ("ctx_0", "ctx_1", "head"))
    in_specs = (
        P(CTX, "head"),
        P(None, CTX, "head"),
        P(None, CTX, "head"),
        P("head", None, CTX),
        P(CTX, "head"),
        P("head", None),
    )
    return jax.shard_map(
        per_device, mesh=finer, in_specs=in_specs, out_specs=P(CTX, "head"), check_vma=False
    )
```

```python
import functools
import jax
import jax.numpy as jnp
from jax import lax
from jax.experimental import pallas as pl
from jax.experimental.pallas import tpu as pltpu
from jax.sharding import Mesh
from jax.sharding import PartitionSpec as P

F32 = jnp.float32
BF16 = jnp.bfloat16
HD = 128
SPAN = 64
CTX = ("ctx_0", "ctx_1")


def dot(a, b):
    return jnp.dot(a, b, preferred_element_type=F32)


def dot_nt(a, b):
    return lax.dot_general(a, b, (((1,), (1,)), ((), ())), preferred_element_type=F32)


def split(x):
    hi = x.astype(BF16)
    return hi, (x - hi.astype(F32)).astype(BF16)


def wide(x):
    return jnp.concatenate(split(x), axis=1)


def square(pair):
    return jnp.concatenate([pair, pair], axis=0)


def halves(x):
    n = x.shape[1] // 2
    return x[:, :n] + x[:, n:]


def read_block(ref, blk, h):
    rows = [
        (j, pl.ds(pl.multiple_of(blk * SPAN + 16 * g, 16), 16))
        for g in range(SPAN // 16)
        for j in range(2)
    ]
    cols = slice(h * HD, (h + 1) * HD)
    return jnp.concatenate([ref[j, r, cols] for j, r in rows], axis=0)


def order(p):
    return (p & ~31) + 2 * (p & 15) + ((p >> 4) & 1)


def map_kernel(
    group, k_hbm, v_hbm, b_hbm, ab_ref, x_ref, e_ref, a_ref, c_ref, k_ref, v_ref, b_ref, lev_ref, sems
):
    copies = [pltpu.make_async_copy(b_hbm, b_ref, sems.at[0])]
    piece = k_ref.shape[1] // 4
    for source, target in ((k_hbm, k_ref), (v_hbm, v_ref)):
        for j in range(2):
            for i in range(4):
                part = (j, slice(i * piece, (i + 1) * piece))
                at = sems.at[len(copies)]
                copies.append(pltpu.make_async_copy(source.at[part], target.at[part], at))
    for copy in copies:
        copy.start()
    heads = k_ref.shape[2] // HD
    blocks = k_ref.shape[1] // SPAN
    sub = 2 * SPAN
    place_r = lax.broadcasted_iota(jnp.int32, (sub, sub), 0)
    place_c = lax.broadcasted_iota(jnp.int32, (sub, sub), 1)
    s_r, s_c = order(place_r), order(place_c)
    apart = s_r ^ s_c
    level = jnp.zeros((sub, sub), jnp.int32)
    for bit in range(1, 7):
        level = level + (apart >= 2**bit).astype(jnp.int32)
    lev_ref[...] = jnp.where(s_r > s_c, level, -1)
    eye = (place_r == place_c).astype(F32)
    for copy in copies[: len(copies) // 2 + 1]:
        copy.wait()

    blocks_of = [[] for _ in range(heads)]
    for step in range(blocks // group):
        probs = [(step * group + i, h) for i in range(group) for h in range(heads)]
        kb = [read_block(k_ref, blk, h) for blk, h in probs]
        num = range(len(probs))
        n, e, N, X = [], [], [], []
        for i in num:
            blk, h = probs[i]
            gram = dot_nt(kb[i], kb[i])
            n2 = jnp.sum(gram * eye, axis=0, keepdims=True) + 1e-6
            first = blk * SPAN
            beta = jnp.concatenate(
                [
                    b_ref[h, j : j + 1, first + 16 * g : first + 16 * (g + 1)]
                    for g in range(SPAN // 16)
                    for j in range(2)
                ],
                axis=1,
            )
            e.append(beta / n2)
            n.append(jnp.sqrt(n2))
            e_ref[h * blocks + blk] = jnp.concatenate([e[i], n[i]], axis=0)
            N.append(jnp.where(lev_ref[...] >= 0, gram * e[i], 0.0))
            X.append(eye - jnp.where(lev_ref[...] == 0, N[i], 0.0))
        for lev in range(1, 7):
            xw = [wide(x) for x in X]
            Z = []
            for i in num:
                C = jnp.where(lev_ref[...] == lev, N[i], 0.0)
                Z.append(halves(dot(wide(C), square(xw[i]))))
            for i in num:
                X[i] = X[i] - halves(dot(xw[i], square(wide(Z[i]))))
        if step == 0:
            for copy in copies[len(copies) // 2 + 1 :]:
                copy.wait()
        A, B = [], []
        for i in num:
            blk, h = probs[i]
            xw = wide(X[i])
            x_ref[h * blocks + blk] = xw
            ke = wide(kb[i].T.astype(F32) * e[i])
            y = halves(dot(ke, square(xw)))
            A.append(wide(eye - dot(wide(y), square(kb[i]))))
            B.append(dot(wide(y * n[i]), square(read_block(v_ref, blk, h))))
        for i in num:
            blk, h = probs[i]
            a_ref[h * blocks + blk] = A[i]
            c_ref[h * blocks + blk] = B[i]
            blocks_of[h].append((A[i], B[i]))

    while len(blocks_of[0]) > 1:
        blocks_of = [
            [joined(maps[i + 1], maps[i]) for i in range(0, len(maps), 2)] for maps in blocks_of
        ]
    for h in range(heads):
        a, c = blocks_of[h][0]
        ab_ref[h] = jnp.concatenate([a[:, :HD], c.astype(BF16)], axis=1)


def joined(later, earlier):
    left, source = later
    b_hi, b_lo = split(earlier[1])
    hi = jnp.concatenate([earlier[0][:, :HD], b_hi], axis=1)
    lo = jnp.concatenate([earlier[0][:, HD:], b_lo], axis=1)
    new = dot(left, square(hi)) + dot(left[:, :HD], lo)
    return wide(new[:, :HD]), new[:, HD:] + source


def local_maps(k, v, betas, group):
    _, tok, cols = k.shape
    heads = cols // HD
    count = heads * tok // SPAN
    return pl.pallas_call(
        functools.partial(map_kernel, group),
        out_shape=(
            jax.ShapeDtypeStruct((heads, HD, 2 * HD), BF16),
            jax.ShapeDtypeStruct((count, 2 * SPAN, 4 * SPAN), BF16),
            jax.ShapeDtypeStruct((count, 2, 2 * SPAN), F32),
            jax.ShapeDtypeStruct((count, HD, 2 * HD), BF16),
            jax.ShapeDtypeStruct((count, HD, HD), F32),
        ),
        in_specs=[pl.BlockSpec(memory_space=pltpu.HBM)] * 3,
        out_specs=[pl.BlockSpec(memory_space=pltpu.VMEM)] * 5,
        scratch_shapes=[
            pltpu.VMEM(k.shape, k.dtype),
            pltpu.VMEM(v.shape, v.dtype),
            pltpu.VMEM(betas.shape, betas.dtype),
            pltpu.VMEM((2 * SPAN, 2 * SPAN), jnp.int32),
            pltpu.SemaphoreType.DMA((17,)),
        ],
        compiler_params=pltpu.CompilerParams(vmem_limit_bytes=16 * 1024 * 1024),
    )(*(pltpu.with_memory_space_constraint(a, pltpu.HBM) for a in (k, v, betas)))


def local_kernel(
    q_hbm,
    k_hbm,
    v_hbm,
    g_hbm,
    x_ref,
    e_ref,
    a_ref,
    c_ref,
    l_ref,
    m_ref,
    s_ref,
    q_ref,
    k_ref,
    v_ref,
    g_ref,
    sems,
):
    copies = []
    cut = q_ref.shape[0] // 2
    for source, target in ((k_hbm, k_ref), (q_hbm, q_ref), (v_hbm, v_ref), (g_hbm, g_ref)):
        for i in range(2):
            rows = slice(i * cut, (i + 1) * cut)
            for part in ((rows,),) if len(source.shape) == 2 else ((0, rows), (1, rows)):
                at = sems.at[len(copies)]
                copies.append(pltpu.make_async_copy(source.at[part], target.at[part], at))
                copies[-1].start()
    for copy in copies:
        copy.wait()
    heads = q_ref.shape[1] // HD
    blocks = q_ref.shape[0] // SPAN
    sub = 2 * SPAN
    seen = (order(lax.broadcasted_iota(jnp.int32, (SPAN, sub), 1)) >> 1) <= lax.broadcasted_iota(
        jnp.int32, (SPAN, sub), 0
    )
    spots = [
        (h * blocks + blk, slice(blk * SPAN, (blk + 1) * SPAN), slice(h * HD, (h + 1) * HD))
        for blk in range(blocks)
        for h in range(heads)
    ]
    num = range(len(spots))
    kb = [read_block(k_ref, i // heads, i % heads) for i in num]
    scores = [
        wide(jnp.where(seen, dot_nt(q_ref[rows, cols], kb[i]), 0.0) * e_ref[at, :1])
        for i, (at, rows, cols) in enumerate(spots)
    ]
    zq = [halves(dot(scores[i], square(x_ref[spots[i][0]]))) for i in num]
    carry = [
        (q_ref[rows, cols].astype(F32) - dot(wide(zq[i]), square(kb[i]))).astype(BF16)
        for i, (_, rows, cols) in enumerate(spots)
    ]
    loc = [
        dot(wide(zq[i] * e_ref[spots[i][0], 1:]), square(read_block(v_ref, i // heads, i % heads)))
        for i in num
    ]
    prefix = {}
    r = lax.broadcasted_iota(jnp.int32, (HD, 2 * HD), 0)
    c = lax.broadcasted_iota(jnp.int32, (HD, 2 * HD), 1)
    state = [(r == c).astype(F32)] * heads
    for i in num:
        at, h = spots[i][0], i % heads
        hi, lo = split(state[h])
        prefix[i] = hi
        if i < len(spots) - heads:
            left = a_ref[at]
            new = dot(left, square(hi)) + dot(left[:, :HD], lo)
            state[h] = jnp.concatenate([new[:, :HD], new[:, HD:] + c_ref[at]], axis=1)
    prod = [dot(carry[i], prefix[i]) for i in num]
    for i, (_, rows, cols) in enumerate(spots):
        qf = q_ref[rows, cols].astype(F32)
        unit = lax.rsqrt(jnp.sum(qf * qf, axis=1, keepdims=True) + 1e-6)
        m_ref[rows, cols] = (prod[i][:, :HD] * unit).astype(BF16)
        l_ref[rows, cols] = (loc[i] + prod[i][:, HD:]) * unit
        gate = g_ref[rows, cols].astype(F32)
        s_ref[rows, cols] = gate / (1.0 + jnp.exp(-gate))


def affine(a, b):
    return jnp.concatenate([a, b], axis=1)


def pair_kernel(x_ref, own_ref, got_ref, send_ref):
    odd = x_ref[0] % 2 == 1
    zero = jnp.zeros((HD, HD), F32)
    for h in range(own_ref.shape[0]):
        own, got = own_ref[h], got_ref[h]
        low, high = jnp.where(odd, got, own), jnp.where(odd, own, got)
        out = dot(high[:, :HD], low) + affine(zero, high[:, HD:].astype(F32))
        send_ref[h] = out.astype(BF16)


def group_kernel(x_ref, own_ref, got_ref, send_ref, tot_ref):
    late = x_ref[0] >= 2
    zero = jnp.zeros((HD, HD), F32)
    for h in range(own_ref.shape[0]):
        own, got = own_ref[h], got_ref[h]
        low, high = jnp.where(late, got, own), jnp.where(late, own, got)
        out = dot(high[:, :HD], low) + affine(zero, high[:, HD:].astype(F32))
        send_ref[h] = out.astype(BF16)
        tot_ref[h] = out


def inside_kernel(x_ref, pair_ref, mate_ref, in_ref):
    late, odd = x_ref[0] >= 2, x_ref[0] % 2 == 1
    r = lax.broadcasted_iota(jnp.int32, (HD, 2 * HD), 0)
    c = lax.broadcasted_iota(jnp.int32, (HD, 2 * HD), 1)
    zero = jnp.zeros((HD, HD), F32)
    for h in range(pair_ref.shape[0]):
        base = jnp.where(late, pair_ref[h], (r == c).astype(BF16))
        map_ = mate_ref[h]
        out = dot(map_[:, :HD], base) + affine(zero, map_[:, HD:].astype(F32))
        in_ref[h] = jnp.where(odd, out, base.astype(F32))


def join_kernel(later_ref, earlier_ref, send_ref, out_ref):
    zero = jnp.zeros((HD, HD), F32)
    for h in range(later_ref.shape[0]):
        later = later_ref[h]
        out = dot(wide(later[:, :HD]), square(earlier_ref[h])) + affine(zero, later[:, HD:])
        send_ref[h] = out.astype(BF16)
        out_ref[h] = out


def carry_kernel(later_ref, earlier_ref, send_ref):
    for h in range(later_ref.shape[0]):
        later = later_ref[h]
        state = dot(wide(later[:, :HD]), square(earlier_ref[h][:, HD:])) + later[:, HD:]
        send_ref[h] = state.astype(BF16)


def entry_kernel(in_ref, near_ref, far_ref, out_ref):
    zero = jnp.zeros((HD, HD), F32)
    for h in range(in_ref.shape[0]):
        near = near_ref[h]
        both = dot(near[:, :HD], far_ref[h]) + affine(zero, near[:, HD:].astype(F32))
        inner = in_ref[h]
        bh, bl = split(both)
        lhs = wide(inner[:, :HD])
        out = dot(lhs, square(bh)) + dot(lhs[:, :HD], bl)
        out_ref[h] = out + affine(zero, inner[:, HD:])


def mix_kernel(entry_ref, state_ref, l_ref, m_ref, s_ref, o_ref):
    for h in range(entry_ref.shape[0]):
        entry = entry_ref[h]
        start = dot(wide(entry[:, :HD]), square(state_ref[h])) + entry[:, HD:]
        cols = slice(h * HD, (h + 1) * HD)
        att = l_ref[:, cols] + dot(m_ref[:, cols], start.astype(BF16))
        scale = lax.rsqrt(jnp.mean(att * att, axis=1, keepdims=True) + 1e-6)
        o_ref[:, cols] = (att * scale * s_ref[:, cols]).astype(BF16)


VM = pl.BlockSpec(memory_space=pltpu.VMEM)
SM = pl.BlockSpec(memory_space=pltpu.SMEM)


def small(kernel, outs, *args, specs=None):
    return pl.pallas_call(
        kernel,
        out_shape=outs,
        in_specs=specs or [VM] * len(args),
        out_specs=jax.tree.map(lambda _: VM, outs),
        compiler_params=pltpu.CompilerParams(vmem_limit_bytes=16 * 1024 * 1024),
    )(*args)


def pack_kernel(chips, me_ref, w_ref, x_ref, ring_ref, sems):
    rows, width = w_ref.shape[0], ring_ref.shape[2]
    chip, core = me_ref[0] // 2, me_ref[0] % 2
    sign = 1 - 2 * (chip % 2)
    half = chips // 2
    hops = [half] + list(range(half - 1, 0, -1)) + list(range(1 - half, 0)) + [0]
    copies = []
    for i, hop in enumerate(hops):
        dest = (chip + chips + sign * hop) % chips
        block = pl.ds(pl.multiple_of((2 * dest + core) * width, width), width)
        for j, source in enumerate((w_ref, x_ref)):
            target = ring_ref.at[i, j * rows : (j + 1) * rows]
            copies.append(pltpu.make_async_copy(source.at[:, block], target, sems.at[2 * i + j]))
            copies[-1].start()
    for copy in copies:
        copy.wait()


def token_parts(big, made):
    tokens = jax.ShapeDtypeStruct(big[0].shape, F32)
    return pl.pallas_call(
        local_kernel,
        out_shape=(tokens, jax.ShapeDtypeStruct(big[0].shape, BF16), tokens),
        in_specs=[pl.BlockSpec(memory_space=pltpu.HBM)] * 4 + [VM] * 4,
        out_specs=(VM, VM, VM),
        scratch_shapes=[pltpu.VMEM(a.shape, a.dtype) for a in big] + [pltpu.SemaphoreType.DMA((12,))],
        compiler_params=pltpu.CompilerParams(vmem_limit_bytes=16 * 1024 * 1024),
    )(*(pltpu.with_memory_space_constraint(a, pltpu.HBM) for a in big), *made)


def pack(chips, me, weight, mate_weight):
    rows = weight.shape[0]
    return pl.pallas_call(
        functools.partial(pack_kernel, chips),
        out_shape=jax.ShapeDtypeStruct((chips, 2 * rows, rows), BF16),
        in_specs=[SM] + [pl.BlockSpec(memory_space=pltpu.HBM)] * 2,
        out_specs=VM,
        scratch_shapes=[pltpu.SemaphoreType.DMA((2 * chips,))],
        compiler_params=pltpu.CompilerParams(vmem_limit_bytes=16 * 1024 * 1024),
    )(me, *(pltpu.with_memory_space_constraint(a, pltpu.HBM) for a in (weight, mate_weight)))


def term(a, b, w):
    rows = a.shape[1]
    return dot(a, w[:rows]) + dot(b, w[rows:])


def far_kernel(me_ref, a_ref, b_ref, w_ref, ahead_ref, back_ref):
    odd = (me_ref[0] // 2) % 2 != 0
    out = term(a_ref[...], b_ref[...], w_ref[0]).astype(BF16)
    cut = ahead_ref.shape[0]
    ahead_ref[...] = jnp.where(odd, out[cut:], out[:cut])
    back_ref[...] = jnp.where(odd, out[:cut], out[cut:])


def hop_kernel(at, side, me_ref, a_ref, b_ref, w_ref, got_ref, o_ref):
    odd = (me_ref[0] // 2) % 2
    out = term(a_ref[...], b_ref[...], w_ref[at])
    cut = got_ref.shape[0]
    for i in range(2):
        rows = slice(i * cut, (i + 1) * cut)
        got = jnp.where((odd + side) % 2 == i, got_ref[...].astype(F32), 0.0)
        o_ref[rows] = (out[rows] + got).astype(BF16)


def rest_kernel(picks, a_ref, b_ref, w_ref, o_ref):
    for i, at in enumerate(picks):
        o_ref[i] = term(a_ref[...], b_ref[...], w_ref[at])


def add_kernel(at, terms_ref, got_ref, o_ref):
    o_ref[...] = (terms_ref[at] + got_ref[...].astype(F32)).astype(o_ref.dtype)


def last_kernel(sum_ref, got_ref, o_ref):
    o_ref[...] = (sum_ref[...] + got_ref[...].astype(F32)).astype(BF16)


def per_device(queries, keys, values, betas, gate, out_weight):
    tok, cols = queries.shape
    heads = cols // HD
    devices = lax.axis_size("head")
    chips = devices // 2
    me = lax.axis_index("head")
    core = me % 2

    def across(a, odd):
        pairs = [(c, (c + 1) % chips) for c in range(odd, chips, 2)]
        both = pairs + [(d, c) for c, d in pairs]
        return lax.ppermute(a, "head", [(2 * c + i, 2 * d + i) for c, d in both for i in range(2)])

    def mate(a):
        return lax.ppermute(a, "head", [(i, i ^ 1) for i in range(devices)])

    def swap_x(a, odd):
        peers = lax.axis_size("ctx_1")
        pairs = [(i, (i + 1) % peers) for i in range(odd, peers, 2)]
        return lax.ppermute(a, "ctx_1", pairs + [(j, i) for i, j in pairs])

    def later_z(a, by):
        groups = lax.axis_size("ctx_0")
        return lax.ppermute(a, "ctx_0", [(i, i + by) for i in range(groups - by)])

    mate_weight = mate(out_weight)
    maps, inverse, scales, lefts, sources = local_maps(keys, values, betas, 8)

    wide_map = jax.ShapeDtypeStruct((heads, HD, 2 * HD), F32)
    wide_send = jax.ShapeDtypeStruct((heads, HD, 2 * HD), BF16)
    state_send = jax.ShapeDtypeStruct((heads, HD, HD), BF16)
    tokens = jax.ShapeDtypeStruct((tok, cols), F32)
    x = lax.axis_index("ctx_1").astype(jnp.int32).reshape(1)
    beside = swap_x(maps, 0)
    pair = small(pair_kernel, wide_send, x, maps, beside, specs=[SM, VM, VM])
    other = swap_x(pair, 1)
    send, total = small(
        group_kernel, (wide_send, wide_map), x, pair, other, specs=[SM, VM, VM]
    )
    inside = small(inside_kernel, wide_map, x, other, beside, specs=[SM, VM, VM])
    near = later_z(send, 1)
    local, carry, silu = token_parts(
        (queries, keys, values, gate), (inverse, scales, lax.optimization_barrier((lefts, total))[0], sources)
    )
    near = lax.optimization_barrier((near, silu))[0]
    send, pair = small(join_kernel, (wide_send, wide_map), total, near)
    far = later_z(send, 2)
    place = me.astype(jnp.int32).reshape(1)
    ring_w = pack(chips, place, out_weight, lax.optimization_barrier((mate_weight, pair))[0])
    far = lax.optimization_barrier((far, ring_w))[0]
    send = small(carry_kernel, state_send, pair, far)
    state = later_z(send, 4)
    entry = small(entry_kernel, wide_map, inside, near, far)
    mixed_in = small(
        mix_kernel,
        jax.ShapeDtypeStruct((tok, cols), BF16),
        entry,
        state,
        local,
        carry,
        silu,
    )
    mate_in = mate(mixed_in)

    half = chips // 2
    sent = jax.ShapeDtypeStruct((tok, cols), BF16)
    part = jax.ShapeDtypeStruct((tok // 2, cols), BF16)
    both = (mixed_in, mate_in, ring_w)
    ahead, back = small(far_kernel, (part, part), place, *both, specs=[SM] + [VM] * 3)
    got, prior, terms = (across(back, 1), across(ahead, 0)), None, None
    for k in range(half - 1, 0, -1):
        sums = [None, None]
        for i in (1, 0) if k % 2 else (0, 1):
            came = got[i]
            if prior is not None:
                came = lax.optimization_barrier((came, prior))[0]
            if k == half - 1:
                body = functools.partial(hop_kernel, 1 + i * (half - 1), i)
                sums[i] = small(body, sent, place, *both, came, specs=[SM] + [VM] * 4)
            else:
                body = functools.partial(add_kernel, 2 * (half - 2 - k) + i)
                sums[i] = small(body, sent, terms, came)
            prior = sums[i]
        if k == half - 1:
            picks = [j + i * (half - 1) for j in range(2, half) for i in range(2)] + [chips - 1]
            terms = small(
                functools.partial(rest_kernel, picks),
                jax.ShapeDtypeStruct((len(picks), tok, cols), F32),
                lax.optimization_barrier((mixed_in, prior))[0],
                mate_in,
                ring_w,
            )
        got = (across(sums[1], 1), across(sums[0], 0))
    came = lax.optimization_barrier((got[0], prior))[0]
    total = small(functools.partial(add_kernel, 2 * half - 4), tokens, terms, came)
    return small(last_kernel, sent, total, got[1])


def solution(mesh):
    z = mesh.shape["ctx"] // 4
    finer = Mesh(mesh.devices.reshape(z, 4, mesh.shape["head"]), ("ctx_0", "ctx_1", "head"))
    in_specs = (
        P(CTX, "head"),
        P(None, CTX, "head"),
        P(None, CTX, "head"),
        P("head", None, CTX),
        P(CTX, "head"),
        P("head", None),
    )
    return jax.shard_map(
        per_device, mesh=finer, in_specs=in_specs, out_specs=P(CTX, "head"), check_vma=False
    )
```

```python
import functools
import jax
import jax.numpy as jnp
from jax import lax
from jax.experimental import pallas as pl
from jax.experimental.pallas import tpu as pltpu
from jax.sharding import Mesh
from jax.sharding import PartitionSpec as P

F32 = jnp.float32
BF16 = jnp.bfloat16
HD = 128
SPAN = 64
CTX = ("ctx_0", "ctx_1")


def dot(a, b):
    return jnp.dot(a, b, preferred_element_type=F32)


def dot_nt(a, b):
    return lax.dot_general(a, b, (((1,), (1,)), ((), ())), preferred_element_type=F32)


def split(x):
    hi = x.astype(BF16)
    return hi, (x - hi.astype(F32)).astype(BF16)


def wide(x):
    return jnp.concatenate(split(x), axis=1)


def square(pair):
    return jnp.concatenate([pair, pair], axis=0)


def halves(x):
    n = x.shape[1] // 2
    return x[:, :n] + x[:, n:]


def read_block(ref, blk, h):
    rows = [
        (j, pl.ds(pl.multiple_of(blk * SPAN + 16 * g, 16), 16))
        for g in range(SPAN // 16)
        for j in range(2)
    ]
    cols = slice(h * HD, (h + 1) * HD)
    return jnp.concatenate([ref[j, r, cols] for j, r in rows], axis=0)


def order(p):
    return (p & ~31) + 2 * (p & 15) + ((p >> 4) & 1)


def map_kernel(
    group, k_hbm, v_hbm, b_hbm, ab_ref, x_ref, e_ref, a_ref, c_ref, k_ref, v_ref, b_ref, lev_ref, sems
):
    copies = [pltpu.make_async_copy(b_hbm, b_ref, sems.at[0])]
    piece = k_ref.shape[1] // 4
    for source, target in ((k_hbm, k_ref), (v_hbm, v_ref)):
        for j in range(2):
            for i in range(4):
                part = (j, slice(i * piece, (i + 1) * piece))
                at = sems.at[len(copies)]
                copies.append(pltpu.make_async_copy(source.at[part], target.at[part], at))
    for copy in copies:
        copy.start()
    heads = k_ref.shape[2] // HD
    blocks = k_ref.shape[1] // SPAN
    sub = 2 * SPAN
    place_r = lax.broadcasted_iota(jnp.int32, (sub, sub), 0)
    place_c = lax.broadcasted_iota(jnp.int32, (sub, sub), 1)
    s_r, s_c = order(place_r), order(place_c)
    apart = s_r ^ s_c
    level = jnp.zeros((sub, sub), jnp.int32)
    for bit in range(1, 7):
        level = level + (apart >= 2**bit).astype(jnp.int32)
    lev_ref[...] = jnp.where(s_r > s_c, level, -1)
    eye = (place_r == place_c).astype(F32)
    for copy in copies[: len(copies) // 2 + 1]:
        copy.wait()

    blocks_of = [[] for _ in range(heads)]
    for step in range(blocks // group):
        probs = [(step * group + i, h) for i in range(group) for h in range(heads)]
        kb = [read_block(k_ref, blk, h) for blk, h in probs]
        num = range(len(probs))
        n, e, N, X = [], [], [], []
        for i in num:
            blk, h = probs[i]
            gram = dot_nt(kb[i], kb[i])
            n2 = jnp.sum(gram * eye, axis=0, keepdims=True) + 1e-6
            first = blk * SPAN
            beta = jnp.concatenate(
                [
                    b_ref[h, j : j + 1, first + 16 * g : first + 16 * (g + 1)]
                    for g in range(SPAN // 16)
                    for j in range(2)
                ],
                axis=1,
            )
            e.append(beta / n2)
            n.append(jnp.sqrt(n2))
            e_ref[h * blocks + blk] = jnp.concatenate([e[i], n[i]], axis=0)
            N.append(jnp.where(lev_ref[...] >= 0, gram * e[i], 0.0))
            X.append(eye - jnp.where(lev_ref[...] == 0, N[i], 0.0))
        for lev in range(1, 7):
            xw = [wide(x) for x in X]
            Z = []
            for i in num:
                C = jnp.where(lev_ref[...] == lev, N[i], 0.0)
                Z.append(halves(dot(wide(C), square(xw[i]))))
            for i in num:
                X[i] = X[i] - halves(dot(xw[i], square(wide(Z[i]))))
        if step == 0:
            for copy in copies[len(copies) // 2 + 1 :]:
                copy.wait()
        A, B = [], []
        for i in num:
            blk, h = probs[i]
            xw = wide(X[i])
            x_ref[h * blocks + blk] = xw
            ke = wide(kb[i].T.astype(F32) * e[i])
            y = halves(dot(ke, square(xw)))
            A.append(wide(eye - dot(wide(y), square(kb[i]))))
            B.append(dot(wide(y * n[i]), square(read_block(v_ref, blk, h))))
        for i in num:
            blk, h = probs[i]
            a_ref[h * blocks + blk] = A[i]
            c_ref[h * blocks + blk] = B[i]
            blocks_of[h].append((A[i], B[i]))

    while len(blocks_of[0]) > 1:
        blocks_of = [
            [joined(maps[i + 1], maps[i]) for i in range(0, len(maps), 2)] for maps in blocks_of
        ]
    for h in range(heads):
        a, c = blocks_of[h][0]
        ab_ref[h] = jnp.concatenate([a[:, :HD], c.astype(BF16)], axis=1)


def joined(later, earlier):
    left, source = later
    b_hi, b_lo = split(earlier[1])
    hi = jnp.concatenate([earlier[0][:, :HD], b_hi], axis=1)
    lo = jnp.concatenate([earlier[0][:, HD:], b_lo], axis=1)
    new = dot(left, square(hi)) + dot(left[:, :HD], lo)
    return wide(new[:, :HD]), new[:, HD:] + source


def local_maps(k, v, betas, group):
    _, tok, cols = k.shape
    heads = cols // HD
    count = heads * tok // SPAN
    return pl.pallas_call(
        functools.partial(map_kernel, group),
        out_shape=(
            jax.ShapeDtypeStruct((heads, HD, 2 * HD), BF16),
            jax.ShapeDtypeStruct((count, 2 * SPAN, 4 * SPAN), BF16),
            jax.ShapeDtypeStruct((count, 2, 2 * SPAN), F32),
            jax.ShapeDtypeStruct((count, HD, 2 * HD), BF16),
            jax.ShapeDtypeStruct((count, HD, HD), F32),
        ),
        in_specs=[pl.BlockSpec(memory_space=pltpu.HBM)] * 3,
        out_specs=[pl.BlockSpec(memory_space=pltpu.VMEM)] * 5,
        scratch_shapes=[
            pltpu.VMEM(k.shape, k.dtype),
            pltpu.VMEM(v.shape, v.dtype),
            pltpu.VMEM(betas.shape, betas.dtype),
            pltpu.VMEM((2 * SPAN, 2 * SPAN), jnp.int32),
            pltpu.SemaphoreType.DMA((17,)),
        ],
        compiler_params=pltpu.CompilerParams(vmem_limit_bytes=16 * 1024 * 1024),
    )(*(pltpu.with_memory_space_constraint(a, pltpu.HBM) for a in (k, v, betas)))


def local_kernel(q_ref, k_ref, v_ref, g_ref, x_ref, e_ref, a_ref, c_ref, l_ref, m_ref, s_ref):
    heads = q_ref.shape[1] // HD
    blocks = q_ref.shape[0] // SPAN
    sub = 2 * SPAN
    seen = (order(lax.broadcasted_iota(jnp.int32, (SPAN, sub), 1)) >> 1) <= lax.broadcasted_iota(
        jnp.int32, (SPAN, sub), 0
    )
    spots = [
        (h * blocks + blk, slice(blk * SPAN, (blk + 1) * SPAN), slice(h * HD, (h + 1) * HD))
        for blk in range(blocks)
        for h in range(heads)
    ]
    num = range(len(spots))
    kb = [read_block(k_ref, i // heads, i % heads) for i in num]
    scores = [
        wide(jnp.where(seen, dot_nt(q_ref[rows, cols], kb[i]), 0.0) * e_ref[at, :1])
        for i, (at, rows, cols) in enumerate(spots)
    ]
    zq = [halves(dot(scores[i], square(x_ref[spots[i][0]]))) for i in num]
    carry = [
        (q_ref[rows, cols].astype(F32) - dot(wide(zq[i]), square(kb[i]))).astype(BF16)
        for i, (_, rows, cols) in enumerate(spots)
    ]
    loc = [
        dot(wide(zq[i] * e_ref[spots[i][0], 1:]), square(read_block(v_ref, i // heads, i % heads)))
        for i in num
    ]
    prefix = {}
    r = lax.broadcasted_iota(jnp.int32, (HD, 2 * HD), 0)
    c = lax.broadcasted_iota(jnp.int32, (HD, 2 * HD), 1)
    state = [(r == c).astype(F32)] * heads
    for i in num:
        at, h = spots[i][0], i % heads
        hi, lo = split(state[h])
        prefix[i] = hi
        if i < len(spots) - heads:
            left = a_ref[at]
            new = dot(left, square(hi)) + dot(left[:, :HD], lo)
            state[h] = jnp.concatenate([new[:, :HD], new[:, HD:] + c_ref[at]], axis=1)
    prod = [dot(carry[i], prefix[i]) for i in num]
    for i, (_, rows, cols) in enumerate(spots):
        qf = q_ref[rows, cols].astype(F32)
        unit = lax.rsqrt(jnp.sum(qf * qf, axis=1, keepdims=True) + 1e-6)
        m_ref[rows, cols] = (prod[i][:, :HD] * unit).astype(BF16)
        l_ref[rows, cols] = (loc[i] + prod[i][:, HD:]) * unit
        gate = g_ref[rows, cols].astype(F32)
        s_ref[rows, cols] = gate / (1.0 + jnp.exp(-gate))


def affine(a, b):
    return jnp.concatenate([a, b], axis=1)


def fold_kernel(x_ref, m_ref, send_ref, tot_ref, in_ref):
    peers, heads = m_ref.shape[:2]
    x = x_ref[0]
    r = lax.broadcasted_iota(jnp.int32, (HD, 2 * HD), 0)
    c = lax.broadcasted_iota(jnp.int32, (HD, 2 * HD), 1)
    zero = jnp.zeros((HD, HD), F32)
    total = [m_ref[0, h].astype(F32) for h in range(heads)]
    inside = [(r == c).astype(F32)] * heads
    for k in range(1, peers):
        for h in range(heads):
            inside[h] = jnp.where(x == k, total[h], inside[h])
            later = m_ref[k, h]
            prod = halves(dot(later[:, :HD], jnp.concatenate(split(total[h]), axis=1)))
            total[h] = prod + affine(zero, later[:, HD:].astype(F32))
    for h in range(heads):
        send_ref[h] = total[h].astype(BF16)
        tot_ref[h] = total[h]
        in_ref[h] = inside[h]


def join_kernel(later_ref, earlier_ref, send_ref, out_ref):
    zero = jnp.zeros((HD, HD), F32)
    for h in range(later_ref.shape[0]):
        later = later_ref[h]
        out = dot(wide(later[:, :HD]), square(earlier_ref[h])) + affine(zero, later[:, HD:])
        send_ref[h] = out.astype(BF16)
        out_ref[h] = out


def carry_kernel(later_ref, earlier_ref, send_ref):
    for h in range(later_ref.shape[0]):
        later = later_ref[h]
        state = dot(wide(later[:, :HD]), square(earlier_ref[h][:, HD:])) + later[:, HD:]
        send_ref[h] = state.astype(BF16)


def entry_kernel(in_ref, near_ref, far_ref, out_ref):
    zero = jnp.zeros((HD, HD), F32)
    for h in range(in_ref.shape[0]):
        near = near_ref[h]
        both = dot(near[:, :HD], far_ref[h]) + affine(zero, near[:, HD:].astype(F32))
        inner = in_ref[h]
        bh, bl = split(both)
        lhs = wide(inner[:, :HD])
        out = dot(lhs, square(bh)) + dot(lhs[:, :HD], bl)
        out_ref[h] = out + affine(zero, inner[:, HD:])


def mix_kernel(entry_ref, state_ref, l_ref, m_ref, s_ref, o_ref):
    for h in range(entry_ref.shape[0]):
        entry = entry_ref[h]
        start = dot(wide(entry[:, :HD]), square(state_ref[h])) + entry[:, HD:]
        cols = slice(h * HD, (h + 1) * HD)
        att = l_ref[:, cols] + dot(m_ref[:, cols], start.astype(BF16))
        scale = lax.rsqrt(jnp.mean(att * att, axis=1, keepdims=True) + 1e-6)
        o_ref[:, cols] = (att * scale * s_ref[:, cols]).astype(BF16)


VM = pl.BlockSpec(memory_space=pltpu.VMEM)
SM = pl.BlockSpec(memory_space=pltpu.SMEM)


def small(kernel, outs, *args, specs=None):
    return pl.pallas_call(
        kernel,
        out_shape=outs,
        in_specs=specs or [VM] * len(args),
        out_specs=jax.tree.map(lambda _: VM, outs),
        compiler_params=pltpu.CompilerParams(vmem_limit_bytes=16 * 1024 * 1024),
    )(*args)


def pack_kernel(chips, me_ref, w_ref, x_ref, ring_ref, sems):
    rows, width = w_ref.shape[0], ring_ref.shape[2]
    chip, core = me_ref[0] // 2, me_ref[0] % 2
    sign = 1 - 2 * (chip % 2)
    half = chips // 2
    hops = [half] + list(range(half - 1, 0, -1)) + list(range(1 - half, 0)) + [0]
    copies = []
    for i, hop in enumerate(hops):
        dest = (chip + chips + sign * hop) % chips
        block = pl.ds(pl.multiple_of((2 * dest + core) * width, width), width)
        for j, source in enumerate((w_ref, x_ref)):
            target = ring_ref.at[i, j * rows : (j + 1) * rows]
            copies.append(pltpu.make_async_copy(source.at[:, block], target, sems.at[2 * i + j]))
            copies[-1].start()
    for copy in copies:
        copy.wait()


def pack(chips, me, weight, mate_weight):
    rows = weight.shape[0]
    return pl.pallas_call(
        functools.partial(pack_kernel, chips),
        out_shape=jax.ShapeDtypeStruct((chips, 2 * rows, rows), BF16),
        in_specs=[SM] + [pl.BlockSpec(memory_space=pltpu.HBM)] * 2,
        out_specs=VM,
        scratch_shapes=[pltpu.SemaphoreType.DMA((2 * chips,))],
        compiler_params=pltpu.CompilerParams(vmem_limit_bytes=16 * 1024 * 1024),
    )(me, *(pltpu.with_memory_space_constraint(a, pltpu.HBM) for a in (weight, mate_weight)))


def term(a, b, w):
    rows = a.shape[1]
    return dot(a, w[:rows]) + dot(b, w[rows:])


def far_kernel(me_ref, a_ref, b_ref, w_ref, ahead_ref, back_ref):
    odd = (me_ref[0] // 2) % 2 != 0
    out = term(a_ref[...], b_ref[...], w_ref[0]).astype(BF16)
    cut = ahead_ref.shape[0]
    ahead_ref[...] = jnp.where(odd, out[cut:], out[:cut])
    back_ref[...] = jnp.where(odd, out[:cut], out[cut:])


def hop_kernel(at, side, me_ref, a_ref, b_ref, w_ref, got_ref, o_ref):
    odd = (me_ref[0] // 2) % 2
    out = term(a_ref[...], b_ref[...], w_ref[at])
    cut = got_ref.shape[0]
    for i in range(2):
        rows = slice(i * cut, (i + 1) * cut)
        got = jnp.where((odd + side) % 2 == i, got_ref[...].astype(F32), 0.0)
        o_ref[rows] = (out[rows] + got).astype(BF16)


def rest_kernel(picks, a_ref, b_ref, w_ref, o_ref):
    for i, at in enumerate(picks):
        o_ref[i] = term(a_ref[...], b_ref[...], w_ref[at])


def add_kernel(at, terms_ref, got_ref, o_ref):
    o_ref[...] = (terms_ref[at] + got_ref[...].astype(F32)).astype(o_ref.dtype)


def last_kernel(sum_ref, got_ref, o_ref):
    o_ref[...] = (sum_ref[...] + got_ref[...].astype(F32)).astype(BF16)


def per_device(queries, keys, values, betas, gate, out_weight):
    tok, cols = queries.shape
    heads = cols // HD
    devices = lax.axis_size("head")
    chips = devices // 2
    me = lax.axis_index("head")
    core = me % 2

    def across(a, odd):
        pairs = [(c, (c + 1) % chips) for c in range(odd, chips, 2)]
        both = pairs + [(d, c) for c, d in pairs]
        return lax.ppermute(a, "head", [(2 * c + i, 2 * d + i) for c, d in both for i in range(2)])

    def mate(a):
        return lax.ppermute(a, "head", [(i, i ^ 1) for i in range(devices)])

    def later_z(a, by):
        groups = lax.axis_size("ctx_0")
        return lax.ppermute(a, "ctx_0", [(i, i + by) for i in range(groups - by)])

    mate_weight = mate(out_weight)
    maps, inverse, scales, lefts, sources = local_maps(keys, values, betas, 8)

    wide_map = jax.ShapeDtypeStruct((heads, HD, 2 * HD), F32)
    wide_send = jax.ShapeDtypeStruct((heads, HD, 2 * HD), BF16)
    state_send = jax.ShapeDtypeStruct((heads, HD, HD), BF16)
    tokens = jax.ShapeDtypeStruct((tok, cols), F32)
    gathered = lax.all_gather(maps, "ctx_1")
    x = lax.axis_index("ctx_1").astype(jnp.int32).reshape(1)
    send, total, inside = small(
        fold_kernel, (wide_send, wide_map, wide_map), x, gathered, specs=[SM, VM]
    )
    near = later_z(send, 1)
    local, carry, silu = small(
        local_kernel,
        (tokens, jax.ShapeDtypeStruct((tok, cols), BF16), tokens),
        queries,
        keys,
        values,
        gate,
        inverse,
        scales,
        lax.optimization_barrier((lefts, total))[0],
        sources,
    )
    near = lax.optimization_barrier((near, silu))[0]
    send, pair = small(join_kernel, (wide_send, wide_map), total, near)
    far = later_z(send, 2)
    place = me.astype(jnp.int32).reshape(1)
    ring_w = pack(chips, place, out_weight, lax.optimization_barrier((mate_weight, pair))[0])
    far = lax.optimization_barrier((far, ring_w))[0]
    send = small(carry_kernel, state_send, pair, far)
    state = later_z(send, 4)
    entry = small(entry_kernel, wide_map, inside, near, far)
    mixed_in = small(
        mix_kernel,
        jax.ShapeDtypeStruct((tok, cols), BF16),
        entry,
        state,
        local,
        carry,
        silu,
    )
    mate_in = mate(mixed_in)

    half = chips // 2
    sent = jax.ShapeDtypeStruct((tok, cols), BF16)
    part = jax.ShapeDtypeStruct((tok // 2, cols), BF16)
    both = (mixed_in, mate_in, ring_w)
    ahead, back = small(far_kernel, (part, part), place, *both, specs=[SM] + [VM] * 3)
    got, prior, terms = (across(back, 1), across(ahead, 0)), None, None
    for k in range(half - 1, 0, -1):
        sums = [None, None]
        for i in (1, 0) if k % 2 else (0, 1):
            came = got[i]
            if prior is not None:
                came = lax.optimization_barrier((came, prior))[0]
            if k == half - 1:
                body = functools.partial(hop_kernel, 1 + i * (half - 1), i)
                sums[i] = small(body, sent, place, *both, came, specs=[SM] + [VM] * 4)
            else:
                body = functools.partial(add_kernel, 2 * (half - 2 - k) + i)
                sums[i] = small(body, sent, terms, came)
            prior = sums[i]
        if k == half - 1:
            picks = [j + i * (half - 1) for j in range(2, half) for i in range(2)] + [chips - 1]
            terms = small(
                functools.partial(rest_kernel, picks),
                jax.ShapeDtypeStruct((len(picks), tok, cols), F32),
                lax.optimization_barrier((mixed_in, prior))[0],
                mate_in,
                ring_w,
            )
        got = (across(sums[1], 1), across(sums[0], 0))
    came = lax.optimization_barrier((got[0], prior))[0]
    total = small(functools.partial(add_kernel, 2 * half - 4), tokens, terms, came)
    return small(last_kernel, sent, total, got[1])


def solution(mesh):
    z = mesh.shape["ctx"] // 4
    finer = Mesh(mesh.devices.reshape(z, 4, mesh.shape["head"]), ("ctx_0", "ctx_1", "head"))
    in_specs = (
        P(CTX, "head"),
        P(None, CTX, "head"),
        P(None, CTX, "head"),
        P("head", None, CTX),
        P(CTX, "head"),
        P("head", None),
    )
    return jax.shard_map(
        per_device, mesh=finer, in_specs=in_specs, out_specs=P(CTX, "head"), check_vma=False
    )
```
